128 devices in a mesh: batch: 8 (over y_lo, x), blk: 16 (over y_hi, z, core).
Axes of the slice: x: 4, y: 4 (y_hi: 2, y_lo: 2; y = y_hi * 2 + y_lo), z: 4, core: 2. Of those that a mesh axis runs over, the one named last changes fastest.
Arguments:
- frames: bfloat16 [16, 2048, 1024], P('batch', 'blk'), may hold values from -6 to 6
- time_embed: bfloat16 [16, 1024], P('batch'), may hold values from -6 to 6
- segments: int32 [16, 2048], P('batch', 'blk'), may hold values from 0 to 5, as said below
- w_mod: bfloat16 [1024, 6144], replicated, may hold values from -0.1875 to 0.1875
- b_mod: bfloat16 [6144], replicated, may hold values from -4 to 4
- w_qkv: bfloat16 [1024, 3072], replicated, may hold values from -0.1875 to 0.1875
- b_qkv: bfloat16 [3072], replicated, may hold values from -4 to 4
- w_out: bfloat16 [1024, 1024], replicated, may hold values from -2 to 2
- b_out: bfloat16 [1024], replicated, may hold values from -6 to 6
- w_up: bfloat16 [1024, 2048], replicated, may hold values from -0.1875 to 0.1875
- b_up: bfloat16 [2048], replicated, may hold values from -4 to 4
- w_down: bfloat16 [2048, 1024], replicated, may hold values from -0.125 to 0.125
- b_down: bfloat16 [1024], replicated, may hold values from -6 to 6
- cotangent: bfloat16 [16, 2048, 1024], P('batch', 'blk'), may hold values from -6 to 6
Outputs:
- out_frames: bfloat16 [16, 2048, 1024], P('batch', 'blk')
- grad_frames: float32 [16, 2048, 1024], P('batch', 'blk')
- grad_time: float32 [16, 1024], P('batch')
- grad_w_mod: float32 [1024, 6144], P(('batch', 'blk'))
- grad_b_mod: float32 [6144], P(('batch', 'blk'))
- grad_w_qkv: float32 [1024, 3072], P(('batch', 'blk'))
- grad_b_qkv: float32 [3072], P(('batch', 'blk'))
- grad_w_out: float32 [1024, 1024], P(('batch', 'blk'))
- grad_b_out: float32 [1024], P(('batch', 'blk'))
- grad_w_up: float32 [1024, 2048], P(('batch', 'blk'))
- grad_b_up: float32 [2048], P(('batch', 'blk'))
- grad_w_down: float32 [2048, 1024], P(('batch', 'blk'))
- grad_b_down: float32 [1024], P(('batch', 'blk'))
The draws below stay inside these ranges and needn't reach their ends.
Inputs may be any that keep to these rules, and one draw needn't show every extreme that they name: Segment numbers start at 0 and never fall along a row. In each aligned group of 2 rows, one row holds segments 0, 1 and 2, with segment 1 beginning within the first 128 frames and ending within the last 128 frames of its row; every other row packs 2 to 6 utterances.
All inputs are finite; a program needn't handle non-finite values.
Results may differ from the reference program's by a relative error of at most 0.018.
Values may be sent and summed in bfloat16 or wider, within the bound.
No kernel may reach another device: no remote copies, remote signals or barrier semaphores. Data moves between devices by JAX's collectives and lax.ppermute only.
A program may use at most 256 MiB of HBM per device.

```python
import math
import jax
import jax.numpy as jnp
from jax import lax

D = 1024
HEADS = 16
FF = 2048
FR_DEV = 128
ROWS_DEV = 2
FRAMES = 2048
ROWS = 16


def draw_segments(key, part):
    pick_key = jax.random.fold_in(key, 21)
    first_key = jax.random.fold_in(key, 22)
    last_key = jax.random.fold_in(key, 23)
    count_key = jax.random.fold_in(key, 24)
    jitter_key = jax.random.fold_in(key, 25)
    group_count = ROWS // ROWS_DEV
    place = jnp.arange(FRAMES, dtype=jnp.int32)[None, :]
    span_pick = jax.random.randint(pick_key, (group_count, 1), 0, ROWS_DEV)
    local_row = jnp.arange(ROWS_DEV, dtype=jnp.int32)[None, :]
    spanning = (local_row == span_pick).reshape(ROWS, 1)
    first = jax.random.randint(first_key, (ROWS, 1), 1, FR_DEV)
    last = jax.random.randint(last_key, (ROWS, 1), FRAMES - FR_DEV + 1, FRAMES)
    span_segment = (place >= first).astype(jnp.int32) + (place >= last).astype(jnp.int32)
    utterances = jax.random.randint(count_key, (ROWS, 1), 2, 7)
    forced_row = (span_pick[0, 0] + 1) % ROWS_DEV
    row_number = jnp.arange(ROWS, dtype=jnp.int32)[:, None]
    utterances = jnp.where(row_number == forced_row, 6, utterances)
    spacing = FRAMES // utterances
    reach = spacing // 4
    raw_draw = jax.random.randint(jitter_key, (ROWS, 5), 0, 1 << 20)
    jitter = raw_draw % (2 * reach + 1) - reach
    cut_index = jnp.arange(5, dtype=jnp.int32)[None, :]
    cuts = jnp.where(cut_index < utterances - 1, (cut_index + 1) * spacing + jitter, FRAMES)
    packed_segment = jnp.sum((place[:, :, None] >= cuts[:, None, :]).astype(jnp.int32), axis=-1)
    return jnp.where(spanning, span_segment, packed_segment).astype(jnp.int32)


def steps_of(key, extent, cuts, least, high):
    factor_of = 1.0
    for dim, shards_of in cuts:
        heights = jax.random.uniform(jax.random.fold_in(jax.random.fold_in(key, 6), dim), (shards_of,), jnp.float32, least / len(cuts), high / len(cuts))
        factor_of = factor_of * jnp.repeat(jnp.exp(heights), extent[dim] // shards_of).reshape((-1,) + (1,) * (len(extent) - 1 - dim))
    return factor_of


def noise(stream_key, extent, scale, bound, pieces=(), kind=jnp.bfloat16):
    drawn = jax.random.normal(stream_key, extent, jnp.float32) * scale
    if len(pieces) > 0:
        drawn = steps_of(stream_key, extent, pieces, -0.22, 0.18) * drawn
    return jnp.clip(drawn, min=-bound, max=bound).astype(kind)


def setup_inputs(seed: int = 0) -> dict:
    seeds = jax.random.split(jax.random.key(seed), 15)
    frames = noise(seeds[0], (ROWS, FRAMES, D), 1.0, 6.0, ((0, 8), (1, 16)))
    time_embed = noise(seeds[1], (ROWS, D), 1.0, 6.0, ((0, 8),))
    segments = draw_segments(jax.random.fold_in(seeds[14], 71), 0)
    w_mod = noise(seeds[3], (D, 6 * D), D ** -0.5, 0.1875)
    b_mod = noise(seeds[4], (6 * D,), 0.3, 4.0)
    w_qkv = noise(seeds[5], (D, 3 * D), D ** -0.5, 0.1875)
    b_qkv = noise(seeds[6], (3 * D,), 0.3, 4.0)
    w_out = noise(seeds[7], (D, D), (D // 128) ** -0.5, 2.0)
    b_out = noise(seeds[8], (D,), 1.0, 6.0)
    w_up = noise(seeds[9], (D, FF), D ** -0.5, 0.1875)
    b_up = noise(seeds[10], (FF,), 0.3, 4.0)
    w_down = noise(seeds[11], (FF, D), FF ** -0.5, 0.125)
    b_down = noise(seeds[12], (D,), 1.0, 6.0)
    cotangent = noise(seeds[13], (ROWS, FRAMES, D), 1.0, 6.0, ((0, 8), (1, 16)))
    return dict(frames=frames, time_embed=time_embed, segments=segments, w_mod=w_mod, b_mod=b_mod, w_qkv=w_qkv, b_qkv=b_qkv, w_out=w_out, b_out=b_out, w_up=w_up, b_up=b_up, w_down=w_down, b_down=b_down, cotangent=cotangent)


EPSILON = 1e-06
MASKED = -1e+30
HIGHEST = lax.Precision.HIGHEST

@jax.custom_vjp
def low(v):
    return lax.optimization_barrier(v.astype(jnp.bfloat16)).astype(jnp.float32)

@jax.custom_vjp
def low_back(v):
    return v

def low_keep(v):
    return (low(v), None)

def low_pass(kept, grad):
    return (grad,)

def back_keep(v):
    return (v, None)

def back_low(kept, grad):
    return (low(grad),)
low.defvjp(low_keep, low_pass)
low_back.defvjp(back_keep, back_low)

def layer_norm(values):
    center = values - lax.optimization_barrier(jnp.mean(values, axis=-1, keepdims=True))
    spread = lax.optimization_barrier(jnp.mean(center * center, axis=-1, keepdims=True))
    return center * lax.rsqrt(spread + EPSILON)

def rotary_tables(position, head_dim):
    half_dim = head_dim // 2
    inverse = jnp.exp(jnp.arange(half_dim, dtype=jnp.float32) * (-2.0 * math.log(10000.0) / head_dim))
    angles = position[:, None] * inverse[None, :]
    angles = jnp.concatenate([angles, angles], axis=-1)
    return (jnp.cos(angles), jnp.sin(angles))

def rotate(values, cosine, sine_table):
    half_dim = values.shape[-1] // 2
    turned = jnp.concatenate([-values[..., half_dim:], values[..., :half_dim]], axis=-1)
    return values * cosine[:, None, :] + turned * sine_table[:, None, :]

def attend(queries, key_rows, value_rows, segment_row):
    frame_total = queries.shape[0]
    head_dim = queries.shape[-1]
    block_rows = math.gcd(512, frame_total)
    block_count = frame_total // block_rows
    query_blocks = queries.reshape(block_count, block_rows, queries.shape[1], head_dim)
    segment_blocks = segment_row.reshape(block_count, block_rows)

    def one_block(pair):
        query_part, segment_part = pair
        scores = jnp.einsum('qhd,khd->hqk', query_part, key_rows, precision=HIGHEST) * head_dim ** (-0.5)
        scores = low_back(scores)
        same_segment = (segment_part[:, None] == segment_row[None, :])[None]
        scores = jnp.where(same_segment, scores, MASKED)
        attn_probs = jax.nn.softmax(scores, axis=-1)
        return jnp.einsum('hqk,khd->qhd', low(attn_probs), value_rows, precision=HIGHEST)
    result = lax.map(jax.checkpoint(one_block), (query_blocks, segment_blocks))
    return result.reshape(frame_total, queries.shape[1], head_dim)

def row_forward(inputs, time_vals, segment_row, params):
    w_mod, b_mod, w_qkv, b_qkv, w_out, b_out, w_up, b_up, w_down, b_down = params
    model_width = inputs.shape[-1]
    head_dim = model_width // HEADS
    time_low = low(jax.nn.silu(time_vals))
    modulation = jnp.dot(time_low, w_mod, precision=HIGHEST) + b_mod
    shift_one, scale_one, gate_one, shift_two, scale_two, gate_two = jnp.split(modulation, 6)
    hidden_one = low(layer_norm(inputs) * (1.0 + scale_one) + shift_one)
    projected = low_back(jnp.dot(hidden_one, w_qkv, precision=HIGHEST) + b_qkv)
    projected = projected.reshape(FRAMES, 3, HEADS, head_dim)
    cosine, sine_table = rotary_tables(jnp.arange(FRAMES, dtype=jnp.float32), head_dim)
    queries = low(rotate(projected[:, 0], cosine, sine_table))
    key_rows = low(rotate(projected[:, 1], cosine, sine_table))
    value_rows = low(projected[:, 2])
    attn_full = attend(queries, key_rows, value_rows, segment_row)
    attn_low = low(low_back(attn_full)).reshape(FRAMES, model_width)
    branch_one = low_back(jnp.dot(attn_low, w_out, precision=HIGHEST) + b_out)
    middle = inputs + gate_one * branch_one
    hidden_two = low(layer_norm(middle) * (1.0 + scale_two) + shift_two)
    up_proj = low_back(jnp.dot(hidden_two, w_up, precision=HIGHEST) + b_up)
    act_low = low(jax.nn.gelu(up_proj, approximate=True))
    branch_two = low_back(jnp.dot(act_low, w_down, precision=HIGHEST) + b_down)
    return middle + gate_two * branch_two

def reference(frames, time_embed, segments, w_mod, b_mod, w_qkv, b_qkv, w_out, b_out, w_up, b_up, w_down, b_down, cotangent):
    params = tuple((weight.astype(jnp.float32) for weight in (w_mod, b_mod, w_qkv, b_qkv, w_out, b_out, w_up, b_up, w_down, b_down)))

    def forward(inputs, time_vals, weights):

        def row_step(carry, packed):
            input_row, time_row, segment_row = packed
            return (carry, row_forward(input_row, time_row, segment_row, weights))
        _, result = lax.scan(row_step, jnp.zeros((), jnp.float32), (inputs, time_vals, segments))
        return result
    output, pullback = jax.vjp(forward, frames.astype(jnp.float32), time_embed.astype(jnp.float32), params)
    grad_inputs, grad_time, grads = pullback(cotangent.astype(jnp.float32))
    return (output.astype(jnp.bfloat16), grad_inputs, grad_time, grads[0], grads[1], grads[2], grads[3], grads[4], grads[5], grads[6], grads[7], grads[8], grads[9])
```

```python
import math

import jax
import jax.numpy as jnp
from jax import lax
from jax.experimental import pallas as pl
from jax.experimental.pallas import tpu as pltpu
from jax.sharding import PartitionSpec as P

BF=jnp.bfloat16; F32=jnp.float32
NEG=-1e30
BQ=256
def pair(ref, j, *idx):
    return jnp.concatenate([ref[(2*j,)+idx], ref[(2*j+1,)+idx]], axis=-1)
def dot(a,b):
    return jnp.dot(a,b,preferred_element_type=F32)
def in_range(i, start, end):
    kpos = i*BQ + lax.broadcasted_iota(jnp.int32,(BQ,BQ),0)
    return (kpos>=start)&(kpos<end)
def three(bounds_ref, r, j, make, carry):
    lo=bounds_ref[r,j,0]; f0=bounds_ref[r,j,1]; f1=bounds_ref[r,j,2]; hi=bounds_ref[r,j,3]
    carry=lax.fori_loop(lo,f0,make(True),carry)
    carry=lax.fori_loop(f0,f1,make(False),carry)
    return lax.fori_loop(f1,hi,make(True),carry)

def fwd_kernel(bounds_ref, qkv_ref, se_ref, o_ref, lse_ref, krow, sref):
    nb=krow.shape[1]
    def rows(r, _):
        def tr(i,_):
            krow[r,i]=pair(qkv_ref,i,r,1).T
            return 0
        lax.fori_loop(0,nb,tr,0)
        def qblock(j,_):
            qT=pair(qkv_ref,j,r,0)
            start=se_ref[r,j,0]; end=se_ref[r,j,1]
            def p1(masked):
                def body(i,m8):
                    s=dot(krow[r,i],qT)
                    if masked: s=jnp.where(in_range(i,start,end),s,NEG)
                    sref[i]=s
                    return jnp.maximum(m8, jnp.max(s.reshape(BQ//8,8,BQ),axis=0))
                return body
            m8=three(bounds_ref,r,j,p1,jnp.full((8,BQ),NEG,F32))
            m=jnp.max(m8,axis=0,keepdims=True)
            def p2(i,c):
                l8,acc=c
                p=jnp.exp(sref[i]-m)
                l8=l8+jnp.sum(p.reshape(BQ//8,8,BQ),axis=0)
                acc=acc+dot(pair(qkv_ref,i,r,2),p.astype(BF))
                return l8,acc
            l8,acc=lax.fori_loop(bounds_ref[r,j,0],bounds_ref[r,j,3],p2,(jnp.zeros((8,BQ),F32),jnp.zeros((64,BQ),F32)))
            l=jnp.sum(l8,axis=0,keepdims=True)
            o=(acc*(1.0/l)).astype(BF)
            o_ref[2*j,r]=o[:,:128]; o_ref[2*j+1,r]=o[:,128:]
            lse_ref[r,j]=m+jnp.log(l)
            return 0
        lax.fori_loop(0,nb,qblock,0)
        return 0
    lax.fori_loop(0,2,rows,0)

def attn_fwd(bounds, qkv, se):
    nb=bounds.shape[1]; ns=qkv.shape[0]
    vm=pl.BlockSpec(memory_space=pltpu.VMEM)
    return pl.pallas_call(fwd_kernel,
        in_specs=[pl.BlockSpec(memory_space=pltpu.SMEM),vm,vm], out_specs=[vm,vm],
        out_shape=[jax.ShapeDtypeStruct((ns,2,64,128),BF), jax.ShapeDtypeStruct((2,nb,1,BQ),F32)],
        scratch_shapes=[pltpu.VMEM((2,nb,BQ,64),BF), pltpu.VMEM((nb,BQ,BQ),F32)],
        compiler_params=pltpu.CompilerParams(vmem_limit_bytes=32<<20),
        cost_estimate=pl.CostEstimate(flops=2*2*2*2048*2048*64,bytes_accessed=3<<20,transcendentals=8<<20),
        name="attn_fwd")(bounds,qkv,se)

def bwd_kernel(bounds_ref, qkv_ref, se_ref, o_ref, g_ref, lse_ref, cs_ref, out_ref, kv, qg, dq, delta):
    nb=kv.shape[0]
    def back(x, i):
        c=pair(cs_ref,i,0); s=pair(cs_ref,i,1)
        a,b=x[:32],x[32:]
        return jnp.concatenate([a*c+b*s, b*c-a*s],axis=0).astype(BF)
    def put(i,r,w,x):
        out_ref[2*i,r,w]=x[:,:128]; out_ref[2*i+1,r,w]=x[:,128:]
    def rows(r,_):
        def prep(i,_):
            kT=pair(qkv_ref,i,r,1); vT=pair(qkv_ref,i,r,2); qT=pair(qkv_ref,i,r,0); gT=pair(g_ref,i,r)
            kv[i]=jnp.concatenate([kT,vT],axis=0).T
            qg[i]=jnp.concatenate([qT,gT],axis=0).T
            delta[i]=jnp.sum(gT.astype(F32)*pair(o_ref,i,r).astype(F32),axis=0,keepdims=True)
            dq[i]=jnp.zeros((64,BQ),F32)
            return 0
        lax.fori_loop(0,nb,prep,0)
        lane=lax.broadcasted_iota(jnp.int32,(BQ,128),1)
        def kblock(i,_):
            kvi=kv[i]
            kT=pair(qkv_ref,i,r,1)
            z=jnp.zeros((64,BQ),BF)
            def make(masked):
                def body(j,c):
                    dk,dv=c
                    qT=pair(qkv_ref,j,r,0); gT=pair(g_ref,j,r)
                    s=dot(kvi,jnp.concatenate([qT,z],axis=0))
                    p=jnp.exp(s-lse_ref[r,j])
                    if masked: p=jnp.where(in_range(i,se_ref[r,j,0],se_ref[r,j,1]),p,0.0)
                    dp=dot(kvi,jnp.concatenate([z,gT],axis=0))
                    ds=(p*(dp-delta[j])).astype(BF)
                    dv=dv+dot(p.astype(BF),qg[j])
                    dk=dk+dot(ds,qg[j])
                    dq[j]=dq[j]+dot(kT,ds)
                    return dk,dv
                return body
            zz=jnp.zeros((BQ,128),F32)
            dk,dv=three(bounds_ref,r,i,make,(zz,zz))
            dkv=jnp.where(lane<64,dk,dv).T
            put(i,r,1,back(dkv[:64],i))
            put(i,r,2,dkv[64:].astype(BF))
            return 0
        lax.fori_loop(0,nb,kblock,0)
        def fin(i,_):
            put(i,r,0,back(dq[i]*0.125,i))
            return 0
        lax.fori_loop(0,nb,fin,0)
        return 0
    lax.fori_loop(0,2,rows,0)

def attn_bwd(bounds, qkv, se, o, g, lse, cs):
    nb=bounds.shape[1]; ns=qkv.shape[0]
    vm=pl.BlockSpec(memory_space=pltpu.VMEM)
    return pl.pallas_call(bwd_kernel,
        in_specs=[pl.BlockSpec(memory_space=pltpu.SMEM)]+[vm]*6, out_specs=vm,
        out_shape=jax.ShapeDtypeStruct((ns,2,3,64,128),BF),
        scratch_shapes=[pltpu.VMEM((nb,BQ,128),BF), pltpu.VMEM((nb,BQ,128),BF), pltpu.VMEM((nb,64,BQ),F32), pltpu.VMEM((nb,1,BQ),F32)],
        compiler_params=pltpu.CompilerParams(vmem_limit_bytes=32<<20),
        cost_estimate=pl.CostEstimate(flops=5*2*2*2048*2048*64,bytes_accessed=6<<20,transcendentals=8<<20),
        name="attn_bwd")(bounds,qkv,se,o,g,lse,cs)

def seg_tables(seg):
    F=seg.shape[1]; nb=F//BQ
    start=jnp.zeros_like(seg); end=jnp.zeros_like(seg)
    for s in range(6):
        below=jnp.sum((seg<s).astype(jnp.int32),axis=1,keepdims=True)
        upto=jnp.sum((seg<=s).astype(jnp.int32),axis=1,keepdims=True)
        start=jnp.where(seg==s,below,start); end=jnp.where(seg==s,upto,end)
    sb=start.reshape(2,nb,BQ); eb=end.reshape(2,nb,BQ)
    lo=sb[:,:,0]//BQ; hi=(eb[:,:,-1]+BQ-1)//BQ
    f0=jnp.clip((sb[:,:,-1]+BQ-1)//BQ,lo,hi); f1=jnp.clip(eb[:,:,0]//BQ,f0,hi)
    bounds=jnp.stack([lo,f0,f1,hi],axis=-1)
    se=jnp.stack([sb,eb],axis=2)[:,:,:,None,:]
    return bounds,se

HEADS = 16
HD = 64
D = 1024
FF = 2048
NB = 8
NK = 16
EPS = 1e-06
FR = 128


def a2a(x, axis):
    return lax.all_to_all(x, axis, 0, 0, tiled=True)


def spread(x, axis):
    n = lax.axis_size(axis)
    return a2a(jnp.broadcast_to(x[None], (n,) + x.shape), axis)


def ln_stats(v):
    center = v - jnp.mean(v, axis=-1, keepdims=True)
    inv = lax.rsqrt(jnp.mean(center * center, axis=-1, keepdims=True) + EPS)
    return center * inv, inv


def ln_back(g, n, inv):
    return inv * (g - jnp.mean(g, axis=-1, keepdims=True) - n * jnp.mean(g * n, axis=-1, keepdims=True))


def dg(a, b, ca, cb):
    return lax.dot_general(a, b, (((ca,), (cb,)), ((), ())), preferred_element_type=F32)


def wgrad_kernel(g_ref, n_ref, w_ref, mod_ref, gw_ref, part_ref, acc, sacc):
    s = pl.program_id(0)

    @pl.when(s == 0)
    def _():
        acc[...] = jnp.zeros_like(acc)
        sacc[...] = jnp.zeros_like(sacc)

    for r in range(2):
        gt = jnp.concatenate([g_ref[0, r], g_ref[1, r]], axis=-1)
        nn = jnp.concatenate([n_ref[0, r], n_ref[1, r]], axis=0)
        acc[r] += dot(gt, nn)
        sacc[r] += jnp.sum(gt.astype(F32), axis=1, keepdims=True)

    @pl.when(s == pl.num_programs(0) - 1)
    def _():
        w = w_ref[...].astype(F32)
        total = jnp.zeros_like(w)
        for r in range(2):
            m = acc[r]
            sv = sacc[r]
            total += m * mod_ref[2 + r : 3 + r] + sv * mod_ref[r : r + 1]
            part_ref[r : r + 1] = jnp.sum(w * sv, axis=0, keepdims=True)
            part_ref[2 + r : 3 + r] = jnp.sum(w * m, axis=0, keepdims=True)
        gw_ref[...] = total.astype(BF)


def wgrad(g, n, wt, mod4):
    ns = g.shape[0]
    return pl.pallas_call(
        wgrad_kernel,
        grid=(ns // 2,),
        in_specs=[
            pl.BlockSpec((2, 2, 192, FR), lambda s: (s, 0, 0, 0)),
            pl.BlockSpec((2, 2, FR, D), lambda s: (s, 0, 0, 0)),
            pl.BlockSpec((192, D), lambda s: (0, 0)),
            pl.BlockSpec((4, D), lambda s: (0, 0)),
        ],
        out_specs=[
            pl.BlockSpec((192, D), lambda s: (0, 0)),
            pl.BlockSpec((4, D), lambda s: (0, 0)),
        ],
        out_shape=[jax.ShapeDtypeStruct((192, D), BF), jax.ShapeDtypeStruct((4, D), F32)],
        scratch_shapes=[pltpu.VMEM((2, 192, D), F32), pltpu.VMEM((2, 192, 1), F32)],
        compiler_params=pltpu.CompilerParams(vmem_limit_bytes=24 << 20),
        cost_estimate=pl.CostEstimate(
            flops=2 * 192 * D * 4096, bytes_accessed=12 << 20, transcendentals=0
        ),
        name="wgrad",
    )(g, n, wt, mod4)


def per_device(
    frames, time_embed, segments, w_mod, b_mod, w_qkv, b_qkv, w_out, b_out,
    w_up, b_up, w_down, b_down, cotangent,
):
    R = frames.shape[0]
    blk = lax.axis_index("blk")
    bat = lax.axis_index("batch")
    me = bat * NK + blk
    seg_all = spread(segments, "blk")
    seg_row = seg_all.transpose(1, 0, 2).reshape(R, NK * FR)
    time_all = spread(time_embed, "batch").reshape(NB * R, D)
    bounds, se = seg_tables(seg_row)
    act_all = jax.nn.silu(time_all.astype(F32)).astype(BF)
    time_vals = time_embed.astype(F32)
    time_act, silu_back = jax.vjp(jax.nn.silu, time_vals)
    time_low = time_act.astype(BF)

    def mod_part(a, b):
        return dg(time_low, w_mod[:, a * D : b * D], 1, 0) + b_mod[a * D : b * D].astype(F32)

    mod_one = mod_part(0, 2)
    shift1, scale1 = mod_one[:, None, :D], mod_one[:, None, D:]
    inputs = frames.astype(F32)
    norm1, inv1 = ln_stats(inputs)
    h1 = (norm1 * (1.0 + scale1) + shift1).astype(BF).reshape(R * FR, D)
    n1_low = norm1.astype(BF)
    inverse = jnp.exp(jnp.arange(32, dtype=F32) * (-2.0 * math.log(10000.0) / HD))
    pos = jnp.arange(NK * FR, dtype=F32).reshape(NK, 1, FR)
    angles = pos * inverse[None, :, None]
    cs = jnp.stack([jnp.cos(angles), jnp.sin(angles)], axis=1)
    cs_me = lax.dynamic_index_in_dim(cs, blk, 0, keepdims=False)
    cosm, sinm = cs_me[0][:, None, :], cs_me[1][:, None, :]

    proj = dg(w_qkv, h1, 0, 1) + b_qkv.astype(F32)[:, None]
    proj = proj.reshape(3, HEADS, 2, 32, R, FR)

    def turn(x, scale):
        a, b = x[:, 0], x[:, 1]
        return jnp.stack([(a * cosm - b * sinm) * scale, (b * cosm + a * sinm) * scale], axis=1)

    qT = turn(proj[0], 0.125).reshape(HEADS, HD, R, FR)
    kT = turn(proj[1], 1.0).reshape(HEADS, HD, R, FR)
    vT = proj[2].reshape(HEADS, HD, R, FR)
    qkvT = jnp.stack([qT, kT, vT], axis=1).astype(BF)
    qkv_send = qkvT.transpose(0, 3, 1, 2, 4)
    qkv = a2a(qkv_send, "blk")

    mod_two = mod_part(2, 6)
    gate1, shift2 = mod_two[:, None, :D], mod_two[:, None, D : 2 * D]
    scale2, gate2 = mod_two[:, None, 2 * D : 3 * D], mod_two[:, None, 3 * D :]
    wt = lax.dynamic_slice_in_dim(w_qkv.reshape(D, 3, HEADS, HD), blk, 1, 2).reshape(D, 192).T

    qkv, n1_gather = lax.optimization_barrier((qkv, n1_low))
    norm_all = lax.all_gather(n1_gather, "blk", axis=0, tiled=False)

    o_heads, lse = attn_fwd(bounds, qkv, se)
    oT = a2a(o_heads, "blk")
    o = oT.transpose(1, 3, 0, 2).reshape(R * FR, D)
    branch1 = (dg(o, w_out, 1, 0) + b_out.astype(F32)).reshape(R, FR, D)
    middle = inputs + gate1 * branch1
    norm2, inv2 = ln_stats(middle)
    h2 = (norm2 * (1.0 + scale2) + shift2).astype(BF).reshape(R * FR, D)
    up = dg(h2, w_up, 1, 0) + b_up.astype(F32)
    gelu_out, gelu_back = jax.vjp(lambda u: jax.nn.gelu(u, approximate=True), up)
    act = gelu_out.astype(BF)
    branch2 = (dg(act, w_down, 1, 0) + b_down.astype(F32)).reshape(R, FR, D)
    output = (middle + gate2 * branch2).astype(BF)
    cot = cotangent.astype(F32)
    g_gate2 = jnp.sum(branch2 * cot, axis=1)
    g_b2 = (gate2 * cot).astype(BF).reshape(R * FR, D)
    (g_up,) = gelu_back(dg(g_b2, w_down, 1, 1))
    g_up = g_up.astype(BF)
    g_h2 = dg(g_up, w_up, 1, 1).reshape(R, FR, D)
    g_scale2 = jnp.sum(g_h2 * norm2, axis=1)
    g_shift2 = jnp.sum(g_h2, axis=1)
    g_middle = cot + ln_back(g_h2 * (1.0 + scale2), norm2, inv2)
    g_gate1 = jnp.sum(branch1 * g_middle, axis=1)
    g_b1 = (gate1 * g_middle).astype(BF).reshape(R * FR, D)
    g_oT = dg(w_out, g_b1, 1, 1).astype(BF).reshape(HEADS, HD, R, FR).transpose(0, 2, 1, 3)
    g_o = a2a(g_oT, "blk")

    gw_down = dg(act, g_b2, 0, 0).reshape(NB, NK, 16, D)
    gw_out = dg(o, g_b1, 0, 0).reshape(NB, NK, 8, D)
    gw_up = dg(h2, g_up, 0, 0).reshape(NB, NK, 8, FF)
    grads = jnp.concatenate([gw_down, gw_out, gw_up[..., :D], gw_up[..., D:]], axis=2).astype(BF)
    grads = grads.transpose(1, 0, 2, 3).reshape(NK * NB * 40, D)
    grads = lax.psum_scatter(grads, "blk", scatter_dimension=0, tiled=True)
    grads = lax.psum_scatter(grads, "batch", scatter_dimension=0, tiled=True).astype(F32)
    grad_w_down = grads[:16]
    grad_w_out = grads[16:24]
    grad_w_up = jnp.concatenate([grads[24:32], grads[32:40]], axis=1)

    part = jnp.concatenate([g_gate1, g_shift2, g_scale2, g_gate2], axis=-1)
    bias = jnp.concatenate(
        [
            jnp.sum(g_b1.astype(F32), axis=0),
            jnp.sum(g_up.astype(F32), axis=0),
            jnp.sum(g_b2.astype(F32), axis=0),
        ]
    )
    early = spread(jnp.concatenate([part.reshape(64, 128), bias.reshape(32, 128)], axis=0), "batch")
    part_rows = early[:, :64].reshape(NB * R, 4 * D)
    bias_sum = jnp.sum(early[:, 64:], axis=0).reshape(8, 512)
    act_mine = lax.dynamic_slice_in_dim(act_all, bat * FR, FR, 1).astype(F32).reshape(NB * R, NK, 8)

    def outer(rows):
        return jnp.einsum("rkd,rc->kdc", act_mine, rows, precision=lax.Precision.HIGHEST)

    def wide(x):
        return jnp.broadcast_to(x.reshape(1, 8, -1), (NK, 8, x.size // 8))

    time_early = dg(part.astype(BF), w_mod[:, 2 * D :], 1, 1)
    pack2 = jnp.concatenate(
        [
            outer(part_rows),
            wide(jnp.sum(part_rows, axis=0)),
            wide(time_early),
            wide(bias_sum),
        ],
        axis=-1,
    ).astype(BF)
    got2 = jnp.sum(a2a(pack2, "blk").astype(F32), axis=0)

    g_qkvT = attn_bwd(bounds, qkv, se, o_heads, g_o, lse, cs)
    g_back = a2a(g_qkvT, "blk")
    mod4 = jnp.concatenate([shift1[:, 0], 1.0 + scale1[:, 0]], axis=0)
    gw_qkv, part4 = wgrad(g_qkvT.reshape(NK, R, 192, FR), norm_all, wt, mod4)
    row_sum = jnp.sum(g_qkvT.astype(F32), axis=(0, 4)).reshape(R, 192)
    s_sum = jnp.sum(row_sum, axis=0)
    part_tail = jnp.concatenate([part4[:2], part4[2:]], axis=-1)
    time_tail = dg(part_tail.astype(BF), w_mod[:, : 2 * D], 1, 1)
    small = jnp.concatenate([part_tail.reshape(-1), jnp.pad(s_sum, (0, 832))]).reshape(40, FR)
    send_b = jnp.concatenate(
        [
            gw_qkv.reshape(192, NB, FR).transpose(1, 0, 2),
            jnp.broadcast_to(small[None].astype(BF), (NB, 40, FR)),
        ],
        axis=1,
    )
    got_b = a2a(send_b, "batch")
    gw_mine = jnp.sum(got_b[:, :192].astype(F32), axis=0)
    tail_rows = got_b[:, 192:224].astype(F32).reshape(NB * R, 2 * D)
    s_all = jnp.sum(got_b[:, 224:232].astype(F32), axis=0).reshape(-1)[:192]
    pack3 = jnp.concatenate(
        [
            outer(tail_rows),
            wide(jnp.sum(tail_rows, axis=0)),
            wide(time_tail),
            gw_mine.T.reshape(NK, 8, 192),
            wide(jnp.pad(s_all, (0, 320))),
        ],
        axis=-1,
    ).astype(BF)
    got3 = a2a(pack3, "blk")
    head_part = got3[:, :, 2 * D :]
    sum3 = jnp.sum(got3[:, :, : 2 * D + 512].astype(F32), axis=0)
    gq = head_part[:, :, 512:704].astype(F32).reshape(NK, 8, 3, HD)
    grad_w_qkv = gq.transpose(1, 2, 0, 3).reshape(8, 3 * D)
    bq = head_part[:, :, 704:768].astype(F32).reshape(NK, 512)[:, :192].reshape(NK, 3, HD)
    b_qkv_sum = bq.transpose(1, 0, 2).reshape(3 * D)
    grad_b_qkv = lax.dynamic_slice_in_dim(b_qkv_sum, me * 24, 24)

    grad_w_mod = jnp.concatenate([sum3[:, : 2 * D], got2[:, : 4 * D]], axis=1)
    b_mod_sum = jnp.concatenate(
        [sum3[:, 2 * D : 2 * D + 256].reshape(-1), got2[:, 4 * D : 4 * D + 512].reshape(-1)]
    )
    grad_b_mod = lax.dynamic_slice_in_dim(b_mod_sum, me * 48, 48)
    time_total = (
        sum3[:, 2 * D + 256 : 2 * D + 512].reshape(R, D)
        + got2[:, 4 * D + 512 : 4 * D + 768].reshape(R, D)
    )
    (grad_time,) = silu_back(time_total)
    biases = got2[:, 4 * D + 768 :].reshape(-1)
    grad_b_out = lax.dynamic_slice_in_dim(biases, me * 8, 8)
    grad_b_up = lax.dynamic_slice_in_dim(biases, D + me * 16, 16)
    grad_b_down = lax.dynamic_slice_in_dim(biases, 3 * D + me * 8, 8)

    gT = g_back.transpose(1, 2, 0, 3, 4).reshape(R, 3 * D, FR)
    g_h1 = lax.dot_general(gT, w_qkv, (((1,), (1,)), ((), ())), preferred_element_type=F32)
    grad_frames = g_middle + ln_back(g_h1 * (1.0 + scale1), norm1, inv1)

    return (
        output, grad_frames, grad_time, grad_w_mod, grad_b_mod, grad_w_qkv, grad_b_qkv,
        grad_w_out, grad_b_out, grad_w_up, grad_b_up, grad_w_down, grad_b_down,
    )


def solution(mesh):
    both = ("batch", "blk")
    return jax.shard_map(
        per_device,
        mesh=mesh,
        in_specs=(
            P("batch", "blk", None), P("batch", None), P("batch", "blk"),
            P(), P(), P(), P(), P(), P(), P(), P(), P(), P(),
            P("batch", "blk", None),
        ),
        out_specs=(
            P("batch", "blk", None), P("batch", "blk", None), P("batch", None),
            P(both, None), P(both), P(both, None), P(both), P(both, None), P(both),
            P(both, None), P(both), P(both, None), P(both),
        ),
        check_vma=False,
    )
```

```python
import math

import jax
import jax.numpy as jnp
from jax import lax
from jax.experimental import pallas as pl
from jax.experimental.pallas import tpu as pltpu
from jax.sharding import PartitionSpec as P

BF=jnp.bfloat16; F32=jnp.float32
NEG=-1e30
US = 1150000000
BQ=256
def pair(ref, j, *idx):
    return jnp.concatenate([ref[(2*j,)+idx], ref[(2*j+1,)+idx]], axis=-1)
def dot(a,b):
    return jnp.dot(a,b,preferred_element_type=F32)
def in_range(i, start, end):
    kpos = i*BQ + lax.broadcasted_iota(jnp.int32,(BQ,BQ),0)
    return (kpos>=start)&(kpos<end)
SEG = 384
GROWS = 416


def at(r, w):
    return pl.ds(pl.multiple_of((r * 3 + w) * 64, 64), 64)


def three(bounds_ref, r, j, make, carry):
    lo=bounds_ref[r,j,0]; f0=bounds_ref[r,j,1]; f1=bounds_ref[r,j,2]; hi=bounds_ref[r,j,3]
    carry=lax.fori_loop(lo,f0,make(True),carry)
    carry=lax.fori_loop(f0,f1,make(False),carry)
    return lax.fori_loop(f1,hi,make(True),carry)

def segment_tables(qkv_ref, bounds_ref, se_ref):
    nb = se_ref.shape[1]
    total = nb * BQ
    for r in range(2):
        rows = [qkv_ref[s, SEG : SEG + 16, :].astype(F32)[r : r + 1] for s in range(2 * nb)]
        seg = jnp.concatenate(rows, axis=0)
        edge = [jnp.int32(0)] + [jnp.sum(jnp.where(seg < s, 1.0, 0.0)).astype(jnp.int32) for s in range(1, 6)]
        edge.append(jnp.int32(total))

        def first_of(p):
            v = edge[0]
            for e in edge[1:]:
                v = jnp.where(e <= p, jnp.maximum(v, e), v)
            return v

        def end_of(p):
            v = edge[-1]
            for e in edge[:-1]:
                v = jnp.where(e > p, jnp.minimum(v, e), v)
            return v

        for j in range(nb):
            p0, p1 = j * BQ, j * BQ + BQ - 1
            lo = first_of(p0) // BQ
            hi = (end_of(p1) + BQ - 1) // BQ
            f0 = jnp.clip((first_of(p1) + BQ - 1) // BQ, lo, hi)
            f1 = jnp.clip(end_of(p0) // BQ, f0, hi)
            for i, v in enumerate((lo, f0, f1, hi)):
                bounds_ref[r, j, i] = v
            here = jnp.concatenate([rows[2 * j], rows[2 * j + 1]], axis=-1)
            start = jnp.zeros((1, BQ), jnp.int32)
            end = jnp.full((1, BQ), edge[1], jnp.int32)
            for s in range(1, 6):
                start = jnp.where(here >= s, edge[s], start)
                end = jnp.where(here >= s, edge[s + 1], end)
            se_ref[r, j, 0] = start
            se_ref[r, j, 1] = end


def fwd_kernel(qkv_ref, o_ref, lse_ref, bounds_ref, se_ref, krow, sref):
    nb=krow.shape[1]
    segment_tables(qkv_ref, bounds_ref, se_ref)
    def rows(r, _):
        def tr(i,_):
            krow[r,i]=pair(qkv_ref,i,at(r,1)).T
            return 0
        lax.fori_loop(0,nb,tr,0)
        def qblock(j,_):
            qT=pair(qkv_ref,j,at(r,0))
            start=se_ref[r,j,0]; end=se_ref[r,j,1]
            def p1(masked):
                def body(i,m8):
                    s=dot(krow[r,i],qT)
                    if masked: s=jnp.where(in_range(i,start,end),s,NEG)
                    sref[i]=s
                    return jnp.maximum(m8, jnp.max(s.reshape(BQ//8,8,BQ),axis=0))
                return body
            m8=three(bounds_ref,r,j,p1,jnp.full((8,BQ),NEG,F32))
            m=jnp.max(m8,axis=0,keepdims=True)
            def p2(i,c):
                l8,acc=c
                p=jnp.exp(sref[i]-m)
                l8=l8+jnp.sum(p.reshape(BQ//8,8,BQ),axis=0)
                acc=acc+dot(pair(qkv_ref,i,at(r,2)),p.astype(BF))
                return l8,acc
            l8,acc=lax.fori_loop(bounds_ref[r,j,0],bounds_ref[r,j,3],p2,(jnp.zeros((8,BQ),F32),jnp.zeros((64,BQ),F32)))
            l=jnp.sum(l8,axis=0,keepdims=True)
            o=(acc*(1.0/l)).astype(BF)
            o_ref[2*j,r]=o[:,:128]; o_ref[2*j+1,r]=o[:,128:]
            lse_ref[r,j]=m+jnp.log(l)
            return 0
        lax.fori_loop(0,nb,qblock,0)
        return 0
    lax.fori_loop(0,2,rows,0)

def attn_fwd(qkv):
    ns=qkv.shape[0]; nb=ns//2
    vm=pl.BlockSpec(memory_space=pltpu.VMEM)
    return pl.pallas_call(fwd_kernel,
        in_specs=[vm], out_specs=[vm,vm,pl.BlockSpec(memory_space=pltpu.SMEM),vm],
        out_shape=[jax.ShapeDtypeStruct((ns,2,64,128),BF), jax.ShapeDtypeStruct((2,nb,1,BQ),F32),
                   jax.ShapeDtypeStruct((2,nb,4),jnp.int32), jax.ShapeDtypeStruct((2,nb,2,1,BQ),jnp.int32)],
        scratch_shapes=[pltpu.VMEM((2,nb,BQ,64),BF), pltpu.VMEM((nb,BQ,BQ),F32)],
        compiler_params=pltpu.CompilerParams(vmem_limit_bytes=32<<20),
        cost_estimate=pl.CostEstimate(flops=33 * US,bytes_accessed=3<<20,transcendentals=8<<20),
        name="attn_fwd")(qkv)

def bwd_kernel(bounds_ref, qkv_ref, se_ref, o_ref, g_ref, lse_ref, cs_ref, out_ref, kv, qg, dq, delta):
    nb=kv.shape[0]
    def back(x, i):
        c=pair(cs_ref,i,0); s=pair(cs_ref,i,1)
        a,b=x[:32],x[32:]
        return jnp.concatenate([a*c+b*s, b*c-a*s],axis=0).astype(BF)
    def put(i,r,w,x):
        out_ref[2*i,at(r,w),:]=x[:,:128]; out_ref[2*i+1,at(r,w),:]=x[:,128:]
    def rows(r,_):
        def prep(i,_):
            kT=pair(qkv_ref,i,at(r,1)); vT=pair(qkv_ref,i,at(r,2)); qT=pair(qkv_ref,i,at(r,0)); gT=pair(g_ref,i,pl.ds(pl.multiple_of(r*64,64),64))
            kv[i]=jnp.concatenate([kT,vT],axis=0).T
            qg[i]=jnp.concatenate([qT,gT],axis=0).T
            delta[i]=jnp.sum(gT.astype(F32)*pair(o_ref,i,r).astype(F32),axis=0,keepdims=True)
            dq[i]=jnp.zeros((64,BQ),F32)
            return 0
        lax.fori_loop(0,nb,prep,0)
        lane=lax.broadcasted_iota(jnp.int32,(BQ,128),1)
        def kblock(i,_):
            kvi=kv[i]
            kT=pair(qkv_ref,i,at(r,1))
            z=jnp.zeros((64,BQ),BF)
            def make(masked):
                def body(j,c):
                    dk,dv=c
                    qT=pair(qkv_ref,j,at(r,0)); gT=pair(g_ref,j,pl.ds(pl.multiple_of(r*64,64),64))
                    s=dot(kvi,jnp.concatenate([qT,z],axis=0))
                    p=jnp.exp(s-lse_ref[r,j])
                    if masked: p=jnp.where(in_range(i,se_ref[r,j,0],se_ref[r,j,1]),p,0.0)
                    dp=dot(kvi,jnp.concatenate([z,gT],axis=0))
                    ds=(p*(dp-delta[j])).astype(BF)
                    dv=dv+dot(p.astype(BF),qg[j])
                    dk=dk+dot(ds,qg[j])
                    dq[j]=dq[j]+dot(kT,ds)
                    return dk,dv
                return body
            zz=jnp.zeros((BQ,128),F32)
            dk,dv=three(bounds_ref,r,i,make,(zz,zz))
            dkv=jnp.where(lane<64,dk,dv).T
            put(i,r,1,back(dkv[:64],i))
            put(i,r,2,dkv[64:].astype(BF))
            return 0
        lax.fori_loop(0,nb,kblock,0)
        def fin(i,_):
            put(i,r,0,back(dq[i]*0.125,i))
            return 0
        lax.fori_loop(0,nb,fin,0)
        return 0
    lax.fori_loop(0,2,rows,0)

def attn_bwd(bounds, qkv, se, o, g, lse, cs):
    nb=bounds.shape[1]; ns=qkv.shape[0]
    vm=pl.BlockSpec(memory_space=pltpu.VMEM)
    return pl.pallas_call(bwd_kernel,
        in_specs=[pl.BlockSpec(memory_space=pltpu.SMEM)]+[vm]*6, out_specs=vm,
        out_shape=jax.ShapeDtypeStruct((ns,GROWS,128),BF),
        scratch_shapes=[pltpu.VMEM((nb,BQ,128),BF), pltpu.VMEM((nb,BQ,128),BF), pltpu.VMEM((nb,64,BQ),F32), pltpu.VMEM((nb,1,BQ),F32)],
        compiler_params=pltpu.CompilerParams(vmem_limit_bytes=32<<20),
        cost_estimate=pl.CostEstimate(flops=40 * US,bytes_accessed=6<<20,transcendentals=8<<20),
        name="attn_bwd")(bounds,qkv,se,o,g,lse,cs)


HEADS = 16
HD = 64
D = 1024
FF = 2048
NB = 8
NK = 16
EPS = 1e-06
FR = 128
FC = 512
RT = 32


def nt(a, b):
    return lax.dot_general(a, b, (((1,), (1,)), ((), ())), preferred_element_type=F32)


def normed(x):
    center = x - jnp.mean(x, axis=-1, keepdims=True)
    inv = lax.rsqrt(jnp.mean(center * center, axis=-1, keepdims=True) + EPS)
    return center * inv, inv


def fold(x):
    return jnp.sum(x.reshape(x.shape[0] // 8, 8, x.shape[1]), axis=0)


def row_tiles(body):
    for r in range(2):

        def step(t, _, r=r):
            body(r, pl.ds(pl.multiple_of(r * FR + t * RT, RT), RT))
            return 0

        lax.fori_loop(0, FR // RT, step, 0)


def pre_kernel(x_ref, mod_ref, wq_ref, wk_ref, wv_ref, bq_ref, bk_ref, bv_ref, cs_ref, seg_ref, send_ref, n1_ref, h1):
    @pl.when(pl.program_id(0) == 0)
    def _():
        def body(r, rows):
            n, _ = normed(x_ref[rows, :].astype(F32))
            n1_ref[rows, :] = n.astype(BF)
            h1[rows, :] = (n * (1.0 + mod_ref[r : r + 1, D:]) + mod_ref[r : r + 1, :D]).astype(BF)

        row_tiles(body)

    c = jnp.concatenate([cs_ref[0], cs_ref[0]], axis=-1)
    s = jnp.concatenate([cs_ref[1], cs_ref[1]], axis=-1)
    for w, (w_ref, b_ref) in enumerate(((wq_ref, bq_ref), (wk_ref, bk_ref), (wv_ref, bv_ref))):
        p = (dot(h1[...], w_ref[...]) + b_ref[...].astype(F32)).T
        for h in range(4):
            y = p[h * HD : (h + 1) * HD]
            if w < 2:
                a, b = y[:32], y[32:]
                y = jnp.concatenate([a * c - b * s, b * c + a * s], axis=0)
                if w == 0:
                    y = y * 0.125
            y = y.astype(BF)
            send_ref[h, w * HD : (w + 1) * HD, :] = y[:, :FR]
            send_ref[h, (3 + w) * HD : (4 + w) * HD, :] = y[:, FR:]
    tile = jnp.concatenate([seg_ref[...].astype(F32), jnp.zeros((14, FR), F32)], axis=0).astype(BF)
    for h in range(4):
        send_ref[h, SEG:, :] = tile


def pre(x, mod1, w_qkv, b_qkv, cs_me, segments):
    whole = lambda shape: pl.BlockSpec(shape, lambda g: (0,) * len(shape))
    wb = [pl.BlockSpec((D, 256), lambda g, w=w: (0, 4 * w + g)) for w in range(3)]
    bb = [pl.BlockSpec((1, 256), lambda g, w=w: (0, 4 * w + g)) for w in range(3)]
    return pl.pallas_call(
        pre_kernel,
        grid=(4,),
        in_specs=[whole((256, D)), whole((2, 2 * D))] + wb + bb + [whole((2, 32, FR)), whole((2, FR))],
        out_specs=[pl.BlockSpec((4, SEG + 16, FR), lambda g: (g, 0, 0)), whole((256, D))],
        out_shape=[jax.ShapeDtypeStruct((HEADS, SEG + 16, FR), BF), jax.ShapeDtypeStruct((256, D), BF)],
        scratch_shapes=[pltpu.VMEM((256, D), BF)],
        compiler_params=pltpu.CompilerParams(vmem_limit_bytes=60 << 20),
        cost_estimate=pl.CostEstimate(flops=8 * US, bytes_accessed=9 << 20, transcendentals=0),
        name="pre",
    )(x, mod1, w_qkv, w_qkv, w_qkv, b_qkv, b_qkv, b_qkv, cs_me, segments)


def mid_kernel(
    core_ref, oT_ref, x_ref, cot_ref, mod_ref, bo_ref, bu_ref, bd_ref, wo_hbm, wu_hbm, wd_hbm,
    out_ref, gm_ref, go_ref, a_ref, keep_ref, send_ref,
    wo, wu, wd, b1, mdl, n2, iv, b2, gh2, gb, sums, bsum, sem,
):
    copies = [pltpu.make_async_copy(wo_hbm, wo, sem.at[0])]
    for f in range(4):
        copies.append(pltpu.make_async_copy(wu_hbm.at[:, pl.ds(f * FC, FC)], wu.at[f], sem.at[1 + f]))
        copies.append(pltpu.make_async_copy(wd_hbm.at[pl.ds(f * FC, FC), :], wd.at[f], sem.at[5 + f]))
    for copy in copies:
        copy.start()
    low = core_ref[0] == 0

    def divide(rows, at, g):
        w = g.shape[1] // 2
        a, b = g[:, :w], g[:, w:]
        keep_ref[rows, at : at + w] = jnp.where(low, a, b)
        send_ref[rows, at : at + w] = jnp.where(low, b, a)

    sums[...] = jnp.zeros_like(sums)
    bsum[...] = jnp.zeros_like(bsum)
    o = jnp.concatenate([oT_ref[:, r].reshape(D, FR).T for r in range(2)], axis=0)
    a_ref[:, :D] = o
    copies[0].wait()
    b1[...] = dot(o, wo[...])

    def first(r, rows):
        gate1, shift2 = mod_ref[r : r + 1, :D], mod_ref[r : r + 1, D : 2 * D]
        scale2, gate2 = mod_ref[r : r + 1, 2 * D : 3 * D], mod_ref[r : r + 1, 3 * D :]
        branch = b1[rows, :] + bo_ref[...].astype(F32)
        b1[rows, :] = branch
        middle = x_ref[rows, :].astype(F32) + gate1 * branch
        mdl[rows, :] = middle
        n, inv = normed(middle)
        n2[rows, :] = n
        iv[rows, :] = jnp.broadcast_to(inv, (RT, FR))
        a_ref[rows, D : 2 * D] = (n * (1.0 + scale2) + shift2).astype(BF)
        g = (gate2 * cot_ref[rows, :].astype(F32)).astype(BF)
        gb[rows, :] = g
        divide(rows, 3 * FC, g)
        bsum[:, 3 * D :] += fold(g.astype(F32))

    row_tiles(first)
    for f in range(4):
        copies[1 + 2 * f].wait()
        copies[2 + 2 * f].wait()
        u = dot(a_ref[:, D : 2 * D], wu[f]) + bu_ref[:, f * FC : (f + 1) * FC].astype(F32)
        k = math.sqrt(2.0 / math.pi)
        sq = u * u
        t = jnp.tanh(u * (k + (k * 0.044715) * sq))
        half = 0.5 * (1.0 + t)
        a = (u * half).astype(BF)
        a_ref[:, 2 * D + f * FC : 2 * D + (f + 1) * FC] = a
        slope = half + (0.5 * u) * (1.0 - t * t) * (k + (3.0 * k * 0.044715) * sq)
        gu = (nt(gb[...], wd[f]) * slope).astype(BF)
        at = FC + (f % 2) * FC

        @pl.when(low == (f < 2))
        def _(gu=gu, at=at):
            keep_ref[:, at : at + FC] = gu

        @pl.when(low != (f < 2))
        def _(gu=gu, at=at):
            send_ref[:, at : at + FC] = gu

        bsum[:, D + f * FC : D + (f + 1) * FC] += fold(gu.astype(F32))
        if f == 0:
            b2[...] = dot(a, wd[f])
            gh2[...] = nt(gu, wu[f])
        else:
            b2[...] += dot(a, wd[f])
            gh2[...] += nt(gu, wu[f])

    def last(r, rows):
        gate1, scale2, gate2 = mod_ref[r : r + 1, :D], mod_ref[r : r + 1, 2 * D : 3 * D], mod_ref[r : r + 1, 3 * D :]
        branch = b2[rows, :] + bd_ref[...].astype(F32)
        cot = cot_ref[rows, :].astype(F32)
        out_ref[rows, :] = (mdl[rows, :] + gate2 * branch).astype(BF)
        sums[r, :, 3 * D :] += fold(branch * cot)
        gh, n = gh2[rows, :], n2[rows, :]
        sums[r, :, D : 2 * D] += fold(gh)
        sums[r, :, 2 * D : 3 * D] += fold(gh * n)
        g = gh * (1.0 + scale2)
        back = g - jnp.mean(g, axis=-1, keepdims=True) - n * jnp.mean(g * n, axis=-1, keepdims=True)
        gm = cot + iv[rows, :1] * back
        gm_ref[rows, :] = gm
        sums[r, :, :D] += fold(b1[rows, :] * gm)
        g1 = (gate1 * gm).astype(BF)
        gb[rows, :] = g1
        divide(rows, 0, g1)
        bsum[:, :D] += fold(g1.astype(F32))

    row_tiles(last)
    goT = nt(wo[...], gb[...]).astype(BF)
    part = [jnp.sum(sums[r], axis=0, keepdims=True) for r in range(2)]
    bias = jnp.sum(bsum[...], axis=0, keepdims=True)
    for k in range(NK):
        go_ref[k, 0:HD] = goT[k * HD : (k + 1) * HD, :FR]
        go_ref[k, HD : 2 * HD] = goT[k * HD : (k + 1) * HD, FR:]
        at = lambda v, i: v[:, (2 * k + i) * FR : (2 * k + i + 1) * FR]
        tile = [at(part[0], 0), at(part[0], 1), at(part[1], 0), at(part[1], 1), at(bias, 0), at(bias, 1)]
        go_ref[k, 2 * HD :] = jnp.concatenate(tile + [jnp.zeros((10, FR), F32)], axis=0).astype(BF)


def mid(core, oT, x, cot, mod2, b_out, b_up, b_down, w_out, w_up, w_down):
    vm = pl.BlockSpec(memory_space=pltpu.VMEM)
    hbm = pl.BlockSpec(memory_space=pl.ANY)
    S = jax.ShapeDtypeStruct
    V = pltpu.VMEM
    return pl.pallas_call(
        mid_kernel,
        in_specs=[pl.BlockSpec(memory_space=pltpu.SMEM)] + [vm] * 7 + [hbm] * 3,
        out_specs=[vm] * 6,
        out_shape=[
            S((256, D), BF), S((256, D), F32), S((NK, 144, FR), BF), S((256, 4 * D), BF),
            S((256, 2 * D), BF), S((256, 2 * D), BF),
        ],
        scratch_shapes=[
            V((D, D), BF), V((4, D, FC), BF), V((4, FC, D), BF), V((256, D), F32), V((256, D), F32),
            V((256, D), F32), V((256, FR), F32), V((256, D), F32), V((256, D), F32), V((256, D), BF),
            V((2, 8, 4 * D), F32), V((8, 4 * D), F32), pltpu.SemaphoreType.DMA((9,)),
        ],
        compiler_params=pltpu.CompilerParams(vmem_limit_bytes=48 << 20),
        cost_estimate=pl.CostEstimate(flops=13 * US, bytes_accessed=16 << 20, transcendentals=256 * FF),
        name="mid",
    )(core, oT, x, cot, mod2, b_out, b_up, b_down, w_out, w_up, w_down)


def dw_kernel(oa, ob, ha, hb, aa, ab, ga, gb, out_ref):
    both = lambda a, b: jnp.concatenate([a[...].T, b[...].T], axis=-1)
    frames = lambda i, j: jnp.concatenate([ga[:, i:j], gb[:, i:j]], axis=0)
    out = dot(both(oa, ob), frames(0, FC)).reshape(NK, 8, FC)
    up = dot(both(ha, hb), frames(FC, 3 * FC)).reshape(NK, 8, 2 * FC)
    down = dot(both(aa, ab), frames(3 * FC, 4 * FC)).reshape(NK, 16, FC)
    out_ref[0, :, :, :FC] = down.astype(BF)
    out_ref[0, :, :, FC : 2 * FC] = jnp.concatenate([out, up[..., :FC]], axis=1).astype(BF)
    half = FC // 2
    out_ref[0, :, :, 2 * FC :] = jnp.concatenate([up[..., FC : FC + half], up[..., FC + half :]], axis=1).astype(BF)


def dw(a, a2, g, g2):
    cols = lambda n, first: pl.BlockSpec((256, n), lambda b: (0, first + b))
    whole = pl.BlockSpec((256, 2 * D), lambda b: (0, 0))
    return pl.pallas_call(
        dw_kernel,
        grid=(NB,),
        in_specs=[cols(128, 0)] * 2 + [cols(128, 8)] * 2 + [cols(256, 8)] * 2 + [whole] * 2,
        out_specs=pl.BlockSpec((1, NK, 16, 1280), lambda b: ((b % 4) * 2 + b // 4, 0, 0, 0)),
        out_shape=jax.ShapeDtypeStruct((NB, NK, 16, 1280), BF),
        compiler_params=pltpu.CompilerParams(vmem_limit_bytes=60 << 20),
        cost_estimate=pl.CostEstimate(flops=6 * US, bytes_accessed=12 << 20, transcendentals=0),
        name="dw",
    )(a, a2, a, a2, a, a2, g, g2)


def tail_kernel(g_ref, w_ref, x_ref, gm_ref, mod_ref, out_ref, gh1):
    step = pl.program_id(0)
    acc = None
    for w in range(3):
        g = jnp.concatenate([g_ref[:, (3 * r + w) * HD : (3 * r + w + 1) * HD, :].reshape(D, FR) for r in range(2)], axis=-1)
        t = dot(w_ref[:, w * D : (w + 1) * D], g)
        acc = t if acc is None else acc + t
    gh1[step] = acc.T

    @pl.when(step == pl.num_programs(0) - 1)
    def _():
        def body(r, rows):
            n, inv = normed(x_ref[rows, :].astype(F32))
            g = jnp.concatenate([gh1[i, rows, :] for i in range(4)], axis=-1)
            g = g * (1.0 + mod_ref[r : r + 1, D:])
            back = g - jnp.mean(g, axis=-1, keepdims=True) - n * jnp.mean(g * n, axis=-1, keepdims=True)
            out_ref[rows, :] = gm_ref[rows, :] + inv * back

        row_tiles(body)


def tail(g_back, w_qkv, x, gm, mod1):
    whole = lambda shape: pl.BlockSpec(shape, lambda g: (0,) * len(shape))
    return pl.pallas_call(
        tail_kernel,
        grid=(4,),
        in_specs=[
            whole((HEADS, GROWS, FR)), pl.BlockSpec((256, 3 * D), lambda g: (g, 0)),
            whole((256, D)), whole((256, D)), whole((2, 2 * D)),
        ],
        out_specs=whole((256, D)),
        out_shape=jax.ShapeDtypeStruct((256, D), F32),
        scratch_shapes=[pltpu.VMEM((4, 256, 256), F32)],
        compiler_params=pltpu.CompilerParams(vmem_limit_bytes=60 << 20),
        cost_estimate=pl.CostEstimate(flops=8 * US, bytes_accessed=10 << 20, transcendentals=0),
        name="tail",
    )(g_back, w_qkv, x, gm, mod1)


def wgrad_kernel(blk_ref, g_ref, n_ref, wq_ref, wk_ref, wv_ref, mod_ref, te_ref, gout_ref, gw_ref, s_ref, acc, sacc):
    s = pl.program_id(0)

    @pl.when(s == 0)
    def _():
        acc[...] = jnp.zeros_like(acc)
        sacc[...] = jnp.zeros_like(sacc)

    for r in range(2):
        gt = jnp.concatenate([g_ref[i, r * 192 : (r + 1) * 192, :] for i in range(2)], axis=-1)
        nn = jnp.concatenate([n_ref[i, r * FR : (r + 1) * FR, :] for i in range(2)], axis=0)
        acc[r] += dot(gt, nn)
        sacc[r] += jnp.sum(gt.astype(F32), axis=1, keepdims=True)

    @pl.when(s == pl.num_programs(0) - 1)
    def _():
        even = blk_ref[0] % 2 == 0
        ws = []
        for ref in (wq_ref, wk_ref, wv_ref):
            t = ref[...].astype(F32).T
            ws.append(jnp.where(even, t[:HD], t[HD:]))
        w = jnp.concatenate(ws, axis=0)
        total = jnp.zeros_like(w)
        rows = []
        for r in range(2):
            m, sv = acc[r], sacc[r]
            shift, scale = mod_ref[r : r + 1, :D], mod_ref[r : r + 1, D:]
            total += m * (1.0 + scale) + sv * shift
            rows.append(jnp.concatenate([jnp.sum(w * sv, axis=0, keepdims=True), jnp.sum(w * m, axis=0, keepdims=True)], axis=-1))
        gw_ref[...] = total.T.astype(BF)
        column = jnp.broadcast_to(sacc[0] + sacc[1], (192, FR))
        s_ref[...] = jnp.concatenate([column, jnp.zeros((HD, FR), F32)], axis=0).T[:8]
        for k in range(NK):
            tile = [v[:, k * FR : (k + 1) * FR] for v in rows] + [jnp.zeros((14, FR), F32)]
            gout_ref[k, :16, :] = jnp.concatenate(tile, axis=0).astype(BF)
            gout_ref[k, 16:, :] = te_ref[...]


def wgrad(blk, g, n, w_qkv, mod1, time_early):
    wb = [pl.BlockSpec((D, FR), lambda s, k, w=w: (0, 8 * w + k[0] // 2)) for w in range(3)]
    whole = lambda shape: pl.BlockSpec(shape, lambda s, k: (0,) * len(shape))
    return pl.pallas_call(
        wgrad_kernel,
        grid_spec=pltpu.PrefetchScalarGridSpec(
            num_scalar_prefetch=1,
            grid=(NK // 2,),
            in_specs=[
                pl.BlockSpec((2, SEG, FR), lambda s, k: (s, 0, 0)),
                pl.BlockSpec((2, 256, D), lambda s, k: (s, 0, 0)),
            ] + wb + [whole((2, 2 * D)), whole((16, FR))],
            out_specs=[pl.BlockSpec((NK, 32, FR), lambda s, k: (0, SEG // 32, 0)), whole((D, 192)), whole((8, 256))],
            scratch_shapes=[pltpu.VMEM((2, 192, D), F32), pltpu.VMEM((2, 192, 1), F32)],
        ),
        out_shape=[
            jax.ShapeDtypeStruct((NK, GROWS, FR), BF), jax.ShapeDtypeStruct((D, 192), BF),
            jax.ShapeDtypeStruct((8, 256), F32),
        ],
        input_output_aliases={1: 0},
        compiler_params=pltpu.CompilerParams(vmem_limit_bytes=60 << 20),
        cost_estimate=pl.CostEstimate(flops=9 * US, bytes_accessed=12 << 20, transcendentals=0),
        name="wgrad",
    )(blk, g, n, w_qkv, w_qkv, w_qkv, mod1, time_early)


def a2a(x, axis):
    return lax.all_to_all(x, axis, 0, 0, tiled=True)


def spread(x, axis):
    n = lax.axis_size(axis)
    return a2a(jnp.broadcast_to(x[None], (n,) + x.shape), axis)


def dg(a, b, ca, cb):
    return lax.dot_general(a, b, (((ca,), (cb,)), ((), ())), preferred_element_type=F32)


def to_core(x):
    return lax.ppermute(x, "blk", [(i, i ^ 1) for i in range(NK)])


def after(x, *others):
    return lax.optimization_barrier((x,) + others)[0]


def per_device(
    frames, time_embed, segments, w_mod, b_mod, w_qkv, b_qkv, w_out, b_out,
    w_up, b_up, w_down, b_down, cotangent,
):
    R = frames.shape[0]
    blk = lax.axis_index("blk")
    bat = lax.axis_index("batch")
    core = blk % 2
    me = bat * NK + blk
    x = frames.reshape(R * FR, D)
    time_vals = time_embed.astype(F32)
    time_act, silu_back = jax.vjp(jax.nn.silu, time_vals)
    time_low = time_act.astype(BF)

    def mod_part(a, b):
        return dg(time_low, w_mod[:, a * D : b * D], 1, 0) + b_mod[a * D : b * D].astype(F32)

    mod1 = mod_part(0, 2)
    inverse = jnp.exp(jnp.arange(32, dtype=F32) * (-2.0 * math.log(10000.0) / HD))
    inverse = inverse[:, None]
    mine = (blk * FR + jnp.arange(FR, dtype=jnp.int32)).astype(F32)[None, :]
    cs_me = jnp.stack([jnp.cos(mine * inverse), jnp.sin(mine * inverse)])
    qkv_send, n1 = pre(x, mod1, w_qkv, b_qkv[None], cs_me, segments)
    qkv = a2a(qkv_send, "blk")

    mod2 = mod_part(2, 6)
    pos = jnp.arange(NK * FR, dtype=F32).reshape(NK, 1, FR)
    angles = pos * inverse[None]
    cs = jnp.stack([jnp.cos(angles), jnp.sin(angles)], axis=1)
    w_mod_mine = lax.dynamic_slice_in_dim(w_mod, 2 * D + blk * 256, 256, 1)

    qkv, n1_gather = lax.optimization_barrier((qkv, n1))
    norm_all = lax.all_gather(n1_gather, "blk", axis=0, tiled=False)

    o_heads, lse, bounds, se = attn_fwd(qkv)
    oT = a2a(o_heads, "blk")
    output, g_middle, go_send, a_all, g_keep, g_give = mid(
        core.astype(jnp.int32).reshape(1), oT, x, cotangent.reshape(R * FR, D), mod2, b_out[None], b_up[None], b_down[None], w_out, w_up, w_down
    )
    go = a2a(go_send, "blk")

    a2_all, g2_all = to_core(a_all), to_core(g_give)
    a2_all, g2_all, go, norm_all = lax.optimization_barrier((a2_all, g2_all, go, norm_all))
    dws = dw(a_all, a2_all, g_keep, g2_all)
    x4 = [[4 * y + i for i in range(4)] for y in range(2)]
    dws = lax.psum_scatter(dws.reshape(NB * 256, 1280), "batch", scatter_dimension=0, axis_index_groups=x4, tiled=True)

    early = jnp.sum(go[:, 128:134].astype(F32), axis=0).reshape(3, 256).astype(BF)
    time_early = dg(early[:2], w_mod_mine, 1, 1).astype(BF)

    g_qkvT = attn_bwd(bounds, qkv, se, o_heads, go, lse, cs)
    g_qkvT, gw_qkv, s_rows = wgrad(
        blk.astype(jnp.int32).reshape(1), g_qkvT, norm_all, w_qkv, mod1, time_early.reshape(16, FR)
    )
    dws = after(dws, gw_qkv).reshape(2, NK, 16, 1280)
    g_back = a2a(g_qkvT, "blk")
    tail_mine = jnp.sum(g_back[:, 384:386].astype(F32), axis=0)
    time_early = jnp.sum(g_back[:, 400:416].astype(F32), axis=0).reshape(R, D)

    def rows_of(v, n):
        return jnp.broadcast_to(v.astype(BF).reshape(1, 8, n), (NB * NK, 8, n))

    pack = jnp.concatenate(
        [
            gw_qkv.reshape(NB * NK, 8, 192),
            rows_of(tail_mine, 32),
            rows_of(early, 96),
            rows_of(s_rows[0, :192], 24),
            time_low.reshape(R, NB * NK, 8).transpose(1, 2, 0),
        ],
        axis=-1,
    )
    pack, dws = lax.optimization_barrier((pack, dws))
    dw_got = lax.ppermute(
        lax.dynamic_index_in_dim(dws, 1 - bat // 4, 0, keepdims=False), "batch", [(i, i ^ 4) for i in range(NB)]
    )
    dws = lax.dynamic_index_in_dim(dws, bat // 4, 0, keepdims=False).astype(F32) + dw_got.astype(F32)
    dws = dws.astype(BF)
    g_back = after(g_back, dws)
    got = a2a(pack, ("batch", "blk")).reshape(NB, NK, 8, 346)
    gq = jnp.sum(got[..., :192].astype(F32), axis=0).reshape(NK, 8, 3, HD)
    grad_w_qkv = gq.transpose(1, 2, 0, 3).reshape(8, 3 * D)
    rows_tail = got[..., 192:224].reshape(NB, NK, R, FR).transpose(0, 2, 1, 3).reshape(NB * R, 2 * D)
    vec = got[..., 224:320].reshape(NB, NK, 3, 256)
    rows_early = vec[:, :, :2].transpose(0, 2, 1, 3).reshape(NB * R, 4 * D)
    rows_all = jnp.concatenate([rows_tail, rows_early], axis=1)
    act_mine = got[:, 0, :, 344:].transpose(0, 2, 1).reshape(NB * R, 8)
    grad_w_mod = dg(act_mine, rows_all, 0, 0)
    b_mod_sum = jnp.sum(rows_all.astype(F32), axis=0)
    grad_b_mod = lax.dynamic_slice_in_dim(b_mod_sum, me * 48, 48)
    biases = jnp.sum(vec[:, :, 2].astype(F32), axis=0).reshape(4 * D)
    grad_b_out = lax.dynamic_slice_in_dim(biases, me * 8, 8)
    grad_b_up = lax.dynamic_slice_in_dim(biases, D + me * 16, 16)
    grad_b_down = lax.dynamic_slice_in_dim(biases, 3 * D + me * 8, 8)
    b_qkv_sum = jnp.sum(got[..., 320:344].astype(F32), axis=0).reshape(NK, 3, HD).transpose(1, 0, 2).reshape(3 * D)
    grad_b_qkv = lax.dynamic_slice_in_dim(b_qkv_sum, me * 24, 24)
    rows_mine = lax.dynamic_slice_in_dim(rows_tail, bat * R, R, 0)
    (grad_time,) = silu_back(time_early + dg(rows_mine, w_mod[:, : 2 * D], 1, 1))

    dws = a2a(after(dws, got), "blk").reshape(NK // 2, 2, 16, 1280)
    dws = jnp.sum(dws.astype(F32), axis=0)
    grad_w_down = jnp.concatenate([dws[0, :, :FC], dws[1, :, :FC]], axis=1)
    grad_w_out = jnp.concatenate([dws[0, :8, FC : 2 * FC], dws[1, :8, FC : 2 * FC]], axis=1)
    grad_w_up = jnp.concatenate(
        [v for c in range(2) for v in (dws[c, 8:, FC : 2 * FC], dws[c, :8, 2 * FC :], dws[c, 8:, 2 * FC :])], axis=1
    )

    grad_frames = tail(g_back, w_qkv, x, g_middle, mod1)
    return (
        output.reshape(R, FR, D), grad_frames.reshape(R, FR, D), grad_time, grad_w_mod, grad_b_mod, grad_w_qkv,
        grad_b_qkv, grad_w_out, grad_b_out, grad_w_up, grad_b_up, grad_w_down, grad_b_down,
    )

def solution(mesh):
    both = ("batch", "blk")
    return jax.shard_map(
        per_device,
        mesh=mesh,
        in_specs=(
            P("batch", "blk", None), P("batch", None), P("batch", "blk"),
            P(), P(), P(), P(), P(), P(), P(), P(), P(), P(),
            P("batch", "blk", None),
        ),
        out_specs=(
            P("batch", "blk", None), P("batch", "blk", None), P("batch", None),
            P(both, None), P(both), P(both, None), P(both), P(both, None), P(both),
            P(both, None), P(both), P(both, None), P(both),
        ),
        check_vma=False,
    )
```

```python
import math

import jax
import jax.numpy as jnp
from jax import lax
from jax.experimental import pallas as pl
from jax.experimental.pallas import tpu as pltpu
from jax.sharding import PartitionSpec as P

BF = jnp.bfloat16
F32 = jnp.float32
NEG = -1e30
US = 1150000000
SEG = 384
GROWS = 416
LN = 128
FQ = FK = 2048
BQ = BK = 512


def dot(a, b):
    return jnp.dot(a, b, preferred_element_type=F32)


def nt(a, b):
    return lax.dot_general(a, b, (((1,), (1,)), ((), ())), preferred_element_type=F32)


def at(r, w):
    return pl.ds(pl.multiple_of((r * 3 + w) * 64, 64), 64)


def lanes(ref, j, n, *idx):
    m = n // LN
    return jnp.concatenate([ref[(j * m + i,) + idx] for i in range(m)], axis=-1)


def first_of(edge_ref, r, p):
    v = jnp.int32(0)
    for i in range(1, 6):
        e = edge_ref[r, i]
        v = jnp.where(e <= p, jnp.maximum(v, e), v)
    return v


def end_of(edge_ref, r, p):
    v = edge_ref[r, 6]
    for i in range(1, 6):
        e = edge_ref[r, i]
        v = jnp.where(e > p, jnp.minimum(v, e), v)
    return v


def over_blocks(edge_ref, r, j, size, step, make, carry):
    p0 = j * size
    p1 = p0 + size - 1
    lo = first_of(edge_ref, r, p0) // step
    hi = (end_of(edge_ref, r, p1) + step - 1) // step
    f0 = jnp.clip((first_of(edge_ref, r, p1) + step - 1) // step, lo, hi)
    f1 = jnp.clip(end_of(edge_ref, r, p0) // step, f0, hi)
    carry = lax.fori_loop(lo, f0, make(True), carry)
    carry = lax.fori_loop(f0, f1, make(False), carry)
    return lax.fori_loop(f1, hi, make(True), carry), lo, hi


def in_range(i, nk, start, end):
    kpos = i * nk + lax.broadcasted_iota(jnp.int32, (nk, start.shape[1]), 0)
    return (kpos >= start) & (kpos < end)


def fold8(x, op):
    return op(x.reshape(x.shape[0] // 8, 8, x.shape[1]), axis=0)


def segment_tables(qkv_ref, edge_ref, se_ref):
    ns = se_ref.shape[1]
    for r in range(2):
        rows = [qkv_ref[s, SEG : SEG + 16, :].astype(F32)[r : r + 1] for s in range(ns)]
        seg = jnp.concatenate(rows, axis=0)
        edge = [jnp.int32(0)] + [jnp.sum(jnp.where(seg < s, 1.0, 0.0)).astype(jnp.int32) for s in range(1, 6)]
        edge.append(jnp.int32(ns * LN))
        for i in range(7):
            edge_ref[r, i] = edge[i]
        edge_ref[r, 7] = jnp.int32(0)
        for s in range(ns):
            start = jnp.zeros((1, LN), jnp.int32)
            end = jnp.full((1, LN), edge[1], jnp.int32)
            for i in range(1, 6):
                start = jnp.where(rows[s] >= i, edge[i], start)
                end = jnp.where(rows[s] >= i, edge[i + 1], end)
            se_ref[r, s, 0:1, :] = start
            se_ref[r, s, 1:2, :] = end


def spans(se_ref, r, j, n):
    m = n // LN
    return [jnp.concatenate([se_ref[r, j * m + i, w : w + 1, :] for i in range(m)], axis=-1) for w in range(2)]


def fwd_kernel(qkv_ref, o_ref, lse_ref, edge_ref, se_ref, krow, sref):
    total = qkv_ref.shape[0] * LN
    segment_tables(qkv_ref, edge_ref, se_ref)

    def rows(r, _):
        def tr(i, _):
            krow[i] = lanes(qkv_ref, i, FK, at(r, 1)).T
            return 0

        lax.fori_loop(0, total // FK, tr, 0)

        def qblock(j, _):
            qT = lanes(qkv_ref, j, FQ, at(r, 0))
            start, end = spans(se_ref, r, j, FQ)

            def make(masked):
                def body(i, m8):
                    s = dot(krow[i], qT)
                    if masked:
                        s = jnp.where(in_range(i, FK, start, end), s, NEG)
                    sref[i] = s
                    return jnp.maximum(m8, fold8(s, jnp.max))

                return body

            m8, lo, hi = over_blocks(edge_ref, r, j, FQ, FK, make, jnp.full((8, FQ), NEG, F32))
            m = jnp.max(m8, axis=0, keepdims=True)

            def second(i, c):
                l8, acc = c
                p = jnp.exp(sref[i] - m)
                return l8 + fold8(p, jnp.sum), acc + dot(lanes(qkv_ref, i, FK, at(r, 2)), p.astype(BF))

            l8, acc = lax.fori_loop(lo, hi, second, (jnp.zeros((8, FQ), F32), jnp.zeros((64, FQ), F32)))
            l = jnp.sum(l8, axis=0, keepdims=True)
            o = (acc * (1.0 / l)).astype(BF)
            lse = m + jnp.log(l)
            for i in range(FQ // LN):
                o_ref[j * (FQ // LN) + i, r] = o[:, i * LN : (i + 1) * LN]
                lse_ref[r, j * (FQ // LN) + i] = jnp.broadcast_to(lse[:, i * LN : (i + 1) * LN], (8, LN))
            return 0

        lax.fori_loop(0, total // FQ, qblock, 0)
        return 0

    lax.fori_loop(0, 2, rows, 0)


def attn_fwd(qkv):
    ns = qkv.shape[0]
    vm = pl.BlockSpec(memory_space=pltpu.VMEM)
    S = jax.ShapeDtypeStruct
    return pl.pallas_call(
        fwd_kernel,
        in_specs=[vm],
        out_specs=[vm, vm, pl.BlockSpec(memory_space=pltpu.SMEM), vm],
        out_shape=[S((ns, 2, 64, LN), BF), S((2, ns, 8, LN), F32), S((2, 8), jnp.int32), S((2, ns, 8, LN), jnp.int32)],
        scratch_shapes=[pltpu.VMEM((ns * LN // FK, FK, 64), BF), pltpu.VMEM((ns * LN // FK, FK, FQ), F32)],
        compiler_params=pltpu.CompilerParams(vmem_limit_bytes=56 << 20),
        cost_estimate=pl.CostEstimate(flops=15 * US, bytes_accessed=3 << 20, transcendentals=8 << 20),
        name="attn_fwd",
    )(qkv)


def bwd_kernel(
    edge_ref, blk_ref, qkv_ref, se_ref, o_ref, g_ref, lse_ref, cs_ref, mod_ref, te_ref, act_ref, n_hbm, w_hbm,
    out_ref, gw_ref, kv, dq, delta, norm, wcol, sem,
):
    total = qkv_ref.shape[0] * LN
    half = blk_ref[0] // 2
    copies = [pltpu.make_async_copy(n_hbm, norm, sem.at[0])]
    for w in range(3):
        cols = pl.ds(pl.multiple_of(w * 1024 + half * LN, LN), LN)
        copies.append(pltpu.make_async_copy(w_hbm.at[:, cols], wcol.at[w], sem.at[1 + w]))
    for copy in copies:
        copy.start()

    def at_g(r):
        return pl.ds(pl.multiple_of(r * 64, 64), 64)

    def back(x, i, n):
        c, s = lanes(cs_ref, i, n, 0), lanes(cs_ref, i, n, 1)
        a, b = x[:32], x[32:]
        return jnp.concatenate([a * c + b * s, b * c - a * s], axis=0).astype(BF)

    def put(i, n, r, w, x):
        for p in range(n // LN):
            out_ref[i * (n // LN) + p, at(r, w), :] = x[:, p * LN : (p + 1) * LN]

    def row_of(ref, r, j):
        return jnp.concatenate([ref[r, j * (BQ // LN) + i, 0:1, :] for i in range(BQ // LN)], axis=-1)

    def rows(r, _):
        def prep(i, _):
            gT = g_ref[i, at_g(r), :]
            kv[pl.ds(pl.multiple_of(i * LN, LN), LN), :] = jnp.concatenate([qkv_ref[i, at(r, 1), :], qkv_ref[i, at(r, 2), :]], axis=0).T
            d = jnp.sum(gT.astype(F32) * o_ref[i, r].astype(F32), axis=0, keepdims=True)
            delta[0, i] = jnp.broadcast_to(d, (8, LN))
            return 0

        lax.fori_loop(0, total // LN, prep, 0)

        def zero(j, _):
            dq[j] = jnp.zeros((64, BQ), F32)
            return 0

        lax.fori_loop(0, total // BQ, zero, 0)

        def kblock(i, _):
            kvi = kv[pl.ds(pl.multiple_of(i * BK, BK), BK), :]
            kT = lanes(qkv_ref, i, BK, at(r, 1))
            z = jnp.zeros((64, BQ), BF)

            def make(masked):
                def body(j, c):
                    dk, dv = c
                    qT, gT = lanes(qkv_ref, j, BQ, at(r, 0)), lanes(g_ref, j, BQ, at_g(r))
                    s = dot(kvi, jnp.concatenate([qT, z], axis=0))
                    p = jnp.exp(s - row_of(lse_ref, r, j))
                    if masked:
                        start, end = spans(se_ref, r, j, BQ)
                        p = jnp.where(in_range(i, BK, start, end), p, 0.0)
                    dp = dot(kvi, jnp.concatenate([z, gT], axis=0))
                    ds = (p * (dp - row_of(delta, 0, j))).astype(BF)
                    dv = dv + nt(gT, p.astype(BF))
                    dk = dk + nt(qT, ds)
                    dq[j] = dq[j] + dot(kT, ds)
                    return dk, dv

                return body

            zz = jnp.zeros((64, BK), F32)
            (dk, dv), _, _ = over_blocks(edge_ref, r, i, BK, BQ, make, (zz, zz))
            put(i, BK, r, 1, back(dk, i, BK))
            put(i, BK, r, 2, dv.astype(BF))
            return 0

        lax.fori_loop(0, total // BK, kblock, 0)

        def fin(j, _):
            put(j, BQ, r, 0, back(dq[j] * 0.125, j, BQ))
            return 0

        lax.fori_loop(0, total // BQ, fin, 0)
        return 0

    lax.fori_loop(0, 2, rows, 0)
    for copy in copies:
        copy.wait()
    even = blk_ref[0] % 2 == 0
    ws = []
    for i in range(3):
        t = wcol[i].astype(F32).T
        ws.append(jnp.where(even, t[:64], t[64:]))
    w = jnp.concatenate(ws, axis=0)
    ns = total // LN
    width = w.shape[1]
    grad = jnp.zeros_like(w)
    bias = jnp.zeros((192, 1), F32)
    parts = []
    for r in range(2):
        gt = jnp.concatenate([out_ref[s, r * 192 : (r + 1) * 192, :] for s in range(ns)], axis=-1)
        m = dot(gt, norm[:, r * LN : (r + 1) * LN, :].reshape(total, width))
        sv = jnp.sum(gt.astype(F32), axis=1, keepdims=True)
        bias += sv
        grad += m * (1.0 + mod_ref[r : r + 1, width:]) + sv * mod_ref[r : r + 1, :width]
        parts.append(
            jnp.concatenate([jnp.sum(w * sv, axis=0, keepdims=True), jnp.sum(w * m, axis=0, keepdims=True)], axis=-1)
        )
    gw_ref[:, :192] = grad.T.astype(BF)
    lane = lax.broadcasted_iota(jnp.int32, (8, 64), 1)
    column = jnp.zeros((8, 64), F32)
    for i in range(24):
        column = jnp.where(lane == 2 + i, bias[8 * i : 8 * i + 8], column)
    extra = act_ref[...].astype(F32).reshape(width // 8, 8, 64) + column[None]
    gw_ref[:, 192:256] = extra.reshape(width, 64).astype(BF)
    for k in range(ns):
        mine = [v[:, k * LN : (k + 1) * LN] for v in parts] + [jnp.zeros((14, LN), F32)]
        out_ref[k, SEG : SEG + 16, :] = jnp.concatenate(mine, axis=0).astype(BF)
        out_ref[k, SEG + 16 :, :] = te_ref[...]


def attn_bwd(edges, blk, qkv, se, o, g, lse, cs, mod1, time_early, act, norm, w_qkv):
    ns = qkv.shape[0]
    width = w_qkv.shape[0]
    vm = pl.BlockSpec(memory_space=pltpu.VMEM)
    sm = pl.BlockSpec(memory_space=pltpu.SMEM)
    hbm = pl.BlockSpec(memory_space=pl.ANY)
    V = pltpu.VMEM
    return pl.pallas_call(
        bwd_kernel,
        in_specs=[sm] * 2 + [vm] * 9 + [hbm] * 2,
        out_specs=[vm, vm],
        out_shape=[jax.ShapeDtypeStruct((ns, GROWS, LN), BF), jax.ShapeDtypeStruct((width, 384), BF)],
        scratch_shapes=[
            V((ns * LN, LN), BF), V((ns * LN // BQ, 64, BQ), F32), V((1, ns, 8, LN), F32),
            V(norm.shape, BF), V((3, width, LN), BF), pltpu.SemaphoreType.DMA((4,)),
        ],
        compiler_params=pltpu.CompilerParams(vmem_limit_bytes=56 << 20),
        cost_estimate=pl.CostEstimate(flops=34 * US, bytes_accessed=15 << 20, transcendentals=8 << 20),
        name="attn_bwd",
    )(edges, blk, qkv, se, o, g, lse, cs, mod1, time_early, act, norm, w_qkv)

HEADS = 16
HD = 64
D = 1024
FF = 2048
NB = 8
NK = 16
EPS = 1e-06
FR = 128
FC = 512
RT = 32


def nt(a, b):
    return lax.dot_general(a, b, (((1,), (1,)), ((), ())), preferred_element_type=F32)


def normed(x):
    center = x - jnp.mean(x, axis=-1, keepdims=True)
    inv = lax.rsqrt(jnp.mean(center * center, axis=-1, keepdims=True) + EPS)
    return center * inv, inv


def fold(x):
    return jnp.sum(x.reshape(x.shape[0] // 8, 8, x.shape[1]), axis=0)


def row_tiles(body):
    for r in range(2):

        def step(t, _, r=r):
            body(r, pl.ds(pl.multiple_of(r * FR + t * RT, RT), RT))
            return 0

        lax.fori_loop(0, FR // RT, step, 0)


def pre_kernel(
    x_ref, t_ref, bm_ref, bq_ref, cs_ref, seg_ref, wm_hbm, wq_hbm, send_ref, n1_ref, mod_ref, wm, wq, nf, h1, sem
):
    first = pltpu.make_async_copy(wm_hbm.at[:, pl.ds(0, 2 * D)], wm, sem.at[0])
    first.start()
    copies = [
        pltpu.make_async_copy(wq_hbm.at[:, pl.ds(i * 256, 256)], wq.at[i], sem.at[1 + i]) for i in range(12)
    ]
    for g in range(4):
        for w in range(3):
            copies[4 * w + g].start()

    def normalize(r, rows):
        n, _ = normed(x_ref[rows, :].astype(F32))
        n1_ref[rows, :] = n.astype(BF)
        nf[rows, :] = n

    row_tiles(normalize)
    t = t_ref[...].astype(F32)
    act = (t / (1.0 + jnp.exp(-t))).astype(BF)
    bm, bq = bm_ref[:16, :].astype(F32), bq_ref[...].astype(F32)
    first.wait()
    mod_ref[...] = dot(act, wm[...]) + jnp.concatenate([bm[i : i + 1] for i in range(16)], axis=-1)

    def modulate(r, rows):
        h1[rows, :] = (nf[rows, :] * (1.0 + mod_ref[r : r + 1, D:]) + mod_ref[r : r + 1, :D]).astype(BF)

    row_tiles(modulate)
    c = jnp.concatenate([cs_ref[0], cs_ref[0]], axis=-1)
    s = jnp.concatenate([cs_ref[1], cs_ref[1]], axis=-1)
    tile = jnp.concatenate([seg_ref[...].astype(F32), jnp.zeros((14, FR), F32)], axis=0).astype(BF)
    for g in range(4):
        for w in range(3):
            i = 4 * w + g
            copies[i].wait()
            p = (dot(h1[...], wq[i]) + jnp.concatenate([bq[2 * i : 2 * i + 1], bq[2 * i + 1 : 2 * i + 2]], axis=-1)).T
            for h in range(4):
                y = p[h * HD : (h + 1) * HD]
                if w < 2:
                    a, b = y[:32], y[32:]
                    y = jnp.concatenate([a * c - b * s, b * c + a * s], axis=0)
                    if w == 0:
                        y = y * 0.125
                y = y.astype(BF)
                send_ref[4 * g + h, w * HD : (w + 1) * HD, :] = y[:, :FR]
                send_ref[4 * g + h, (3 + w) * HD : (4 + w) * HD, :] = y[:, FR:]
        for h in range(4):
            send_ref[4 * g + h, SEG:, :] = tile


def pre(x, t, b_mod, b_qkv, cs_me, segments, w_mod, w_qkv):
    vm = pl.BlockSpec(memory_space=pltpu.VMEM)
    hbm = pl.BlockSpec(memory_space=pl.ANY)
    S = jax.ShapeDtypeStruct
    V = pltpu.VMEM
    return pl.pallas_call(
        pre_kernel,
        in_specs=[vm] * 6 + [hbm] * 2,
        out_specs=[vm] * 3,
        out_shape=[S((HEADS, SEG + 16, FR), BF), S((256, D), BF), S((2, 2 * D), F32)],
        scratch_shapes=[V((D, 2 * D), BF), V((12, D, 256), BF), V((256, D), F32), V((256, D), BF), pltpu.SemaphoreType.DMA((13,))],
        compiler_params=pltpu.CompilerParams(vmem_limit_bytes=60 << 20),
        cost_estimate=pl.CostEstimate(flops=8 * US, bytes_accessed=13 << 20, transcendentals=0),
        name="pre",
    )(x, t, b_mod, b_qkv, cs_me, segments, w_mod, w_qkv)


def mid_kernel(
    core_ref, oT_ref, x_ref, cot_ref, mod_ref, bo_ref, bu_ref, bd_ref, wo_hbm, wu_hbm, wd_hbm,
    out_ref, gm_ref, go_ref, a_ref, keep_ref, send_ref,
    wo, wu, wd, b1, mdl, n2, iv, b2, gh2, gb, sums, bsum, sem,
):
    copies = [pltpu.make_async_copy(wo_hbm, wo, sem.at[0])]
    for f in range(4):
        copies.append(pltpu.make_async_copy(wu_hbm.at[:, pl.ds(f * FC, FC)], wu.at[f], sem.at[1 + f]))
        copies.append(pltpu.make_async_copy(wd_hbm.at[pl.ds(f * FC, FC), :], wd.at[f], sem.at[5 + f]))
    for copy in copies:
        copy.start()
    low = core_ref[0] == 0

    def divide(rows, at, g):
        w = g.shape[1] // 2
        a, b = g[:, :w], g[:, w:]
        keep_ref[rows, at : at + w] = jnp.where(low, a, b)
        send_ref[rows, at : at + w] = jnp.where(low, b, a)

    sums[...] = jnp.zeros_like(sums)
    bsum[...] = jnp.zeros_like(bsum)
    o = jnp.concatenate([oT_ref[:, r].reshape(D, FR).T for r in range(2)], axis=0)
    a_ref[:, :D] = o
    copies[0].wait()
    b1[...] = dot(o, wo[...])

    def first(r, rows):
        gate1, shift2 = mod_ref[r : r + 1, :D], mod_ref[r : r + 1, D : 2 * D]
        scale2, gate2 = mod_ref[r : r + 1, 2 * D : 3 * D], mod_ref[r : r + 1, 3 * D :]
        branch = b1[rows, :] + bo_ref[...].astype(F32)
        b1[rows, :] = branch
        middle = x_ref[rows, :].astype(F32) + gate1 * branch
        mdl[rows, :] = middle
        n, inv = normed(middle)
        n2[rows, :] = n
        iv[rows, :] = jnp.broadcast_to(inv, (RT, FR))
        a_ref[rows, D : 2 * D] = (n * (1.0 + scale2) + shift2).astype(BF)
        g = (gate2 * cot_ref[rows, :].astype(F32)).astype(BF)
        gb[rows, :] = g
        divide(rows, 3 * FC, g)
        bsum[:, 3 * D :] += fold(g.astype(F32))

    row_tiles(first)
    for f in range(4):
        copies[1 + 2 * f].wait()
        copies[2 + 2 * f].wait()
        u = dot(a_ref[:, D : 2 * D], wu[f]) + bu_ref[:, f * FC : (f + 1) * FC].astype(F32)
        k = math.sqrt(2.0 / math.pi)
        sq = u * u
        t = jnp.tanh(u * (k + (k * 0.044715) * sq))
        half = 0.5 * (1.0 + t)
        a = (u * half).astype(BF)
        a_ref[:, 2 * D + f * FC : 2 * D + (f + 1) * FC] = a
        slope = half + (0.5 * u) * (1.0 - t * t) * (k + (3.0 * k * 0.044715) * sq)
        gu = (nt(gb[...], wd[f]) * slope).astype(BF)
        at = FC + (f % 2) * FC

        @pl.when(low == (f < 2))
        def _(gu=gu, at=at):
            keep_ref[:, at : at + FC] = gu

        @pl.when(low != (f < 2))
        def _(gu=gu, at=at):
            send_ref[:, at : at + FC] = gu

        bsum[:, D + f * FC : D + (f + 1) * FC] += fold(gu.astype(F32))
        if f == 0:
            b2[...] = dot(a, wd[f])
            gh2[...] = nt(gu, wu[f])
        else:
            b2[...] += dot(a, wd[f])
            gh2[...] += nt(gu, wu[f])

    def last(r, rows):
        gate1, scale2, gate2 = mod_ref[r : r + 1, :D], mod_ref[r : r + 1, 2 * D : 3 * D], mod_ref[r : r + 1, 3 * D :]
        branch = b2[rows, :] + bd_ref[...].astype(F32)
        cot = cot_ref[rows, :].astype(F32)
        out_ref[rows, :] = (mdl[rows, :] + gate2 * branch).astype(BF)
        sums[r, :, 3 * D :] += fold(branch * cot)
        gh, n = gh2[rows, :], n2[rows, :]
        sums[r, :, D : 2 * D] += fold(gh)
        sums[r, :, 2 * D : 3 * D] += fold(gh * n)
        g = gh * (1.0 + scale2)
        back = g - jnp.mean(g, axis=-1, keepdims=True) - n * jnp.mean(g * n, axis=-1, keepdims=True)
        gm = cot + iv[rows, :1] * back
        gm_ref[rows, :] = gm
        sums[r, :, :D] += fold(b1[rows, :] * gm)
        g1 = (gate1 * gm).astype(BF)
        gb[rows, :] = g1
        divide(rows, 0, g1)
        bsum[:, :D] += fold(g1.astype(F32))

    row_tiles(last)
    goT = nt(wo[...], gb[...]).astype(BF)
    part = [jnp.sum(sums[r], axis=0, keepdims=True) for r in range(2)]
    bias = jnp.sum(bsum[...], axis=0, keepdims=True)
    for k in range(NK):
        go_ref[k, 0:HD] = goT[k * HD : (k + 1) * HD, :FR]
        go_ref[k, HD : 2 * HD] = goT[k * HD : (k + 1) * HD, FR:]
        at = lambda v, i: v[:, (2 * k + i) * FR : (2 * k + i + 1) * FR]
        tile = [at(part[0], 0), at(part[0], 1), at(part[1], 0), at(part[1], 1), at(bias, 0), at(bias, 1)]
        go_ref[k, 2 * HD :] = jnp.concatenate(tile + [jnp.zeros((10, FR), F32)], axis=0).astype(BF)


def mid(core, oT, x, cot, mod2, b_out, b_up, b_down, w_out, w_up, w_down):
    vm = pl.BlockSpec(memory_space=pltpu.VMEM)
    hbm = pl.BlockSpec(memory_space=pl.ANY)
    S = jax.ShapeDtypeStruct
    V = pltpu.VMEM
    return pl.pallas_call(
        mid_kernel,
        in_specs=[pl.BlockSpec(memory_space=pltpu.SMEM)] + [vm] * 7 + [hbm] * 3,
        out_specs=[vm] * 6,
        out_shape=[
            S((256, D), BF), S((256, D), F32), S((NK, 144, FR), BF), S((256, 4 * D), BF),
            S((256, 2 * D), BF), S((256, 2 * D), BF),
        ],
        scratch_shapes=[
            V((D, D), BF), V((4, D, FC), BF), V((4, FC, D), BF), V((256, D), F32), V((256, D), F32),
            V((256, D), F32), V((256, FR), F32), V((256, D), F32), V((256, D), F32), V((256, D), BF),
            V((2, 8, 4 * D), F32), V((8, 4 * D), F32), pltpu.SemaphoreType.DMA((9,)),
        ],
        compiler_params=pltpu.CompilerParams(vmem_limit_bytes=48 << 20),
        cost_estimate=pl.CostEstimate(flops=13 * US, bytes_accessed=16 << 20, transcendentals=256 * FF),
        name="mid",
    )(core, oT, x, cot, mod2, b_out, b_up, b_down, w_out, w_up, w_down)


def dw_kernel(oa, ob, ha, hb, aa, ab, ga, gb, out_ref):
    both = lambda a, b: jnp.concatenate([a[...].T, b[...].T], axis=-1)
    frames = lambda i, j: jnp.concatenate([ga[:, i:j], gb[:, i:j]], axis=0)
    out = dot(both(oa, ob), frames(0, FC)).reshape(NK, 8, FC)
    up = dot(both(ha, hb), frames(FC, 3 * FC)).reshape(NK, 8, 2 * FC)
    down = dot(both(aa, ab), frames(3 * FC, 4 * FC)).reshape(NK, 16, FC)
    out_ref[0, :, :, :FC] = down.astype(BF)
    out_ref[0, :, :, FC : 2 * FC] = jnp.concatenate([out, up[..., :FC]], axis=1).astype(BF)
    half = FC // 2
    out_ref[0, :, :, 2 * FC :] = jnp.concatenate([up[..., FC : FC + half], up[..., FC + half :]], axis=1).astype(BF)


def dw(a, a2, g, g2):
    cols = lambda n, first: pl.BlockSpec((256, n), lambda b: (0, first + b))
    whole = pl.BlockSpec((256, 2 * D), lambda b: (0, 0))
    return pl.pallas_call(
        dw_kernel,
        grid=(NB,),
        in_specs=[cols(128, 0)] * 2 + [cols(128, 8)] * 2 + [cols(256, 8)] * 2 + [whole] * 2,
        out_specs=pl.BlockSpec((1, NK, 16, 1280), lambda b: ((b % 4) * 2 + b // 4, 0, 0, 0)),
        out_shape=jax.ShapeDtypeStruct((NB, NK, 16, 1280), BF),
        compiler_params=pltpu.CompilerParams(vmem_limit_bytes=60 << 20),
        cost_estimate=pl.CostEstimate(flops=6 * US, bytes_accessed=12 << 20, transcendentals=0),
        name="dw",
    )(a, a2, a, a2, a, a2, g, g2)


def tail_kernel(g_ref, w_ref, x_ref, gm_ref, mod_ref, out_ref, gh1):
    step = pl.program_id(0)
    acc = None
    for w in range(3):
        g = jnp.concatenate([g_ref[:, (3 * r + w) * HD : (3 * r + w + 1) * HD, :].reshape(D, FR) for r in range(2)], axis=-1)
        t = dot(w_ref[:, w * D : (w + 1) * D], g)
        acc = t if acc is None else acc + t
    gh1[step] = acc.T

    @pl.when(step == pl.num_programs(0) - 1)
    def _():
        def body(r, rows):
            n, inv = normed(x_ref[rows, :].astype(F32))
            g = jnp.concatenate([gh1[i, rows, :] for i in range(4)], axis=-1)
            g = g * (1.0 + mod_ref[r : r + 1, D:])
            back = g - jnp.mean(g, axis=-1, keepdims=True) - n * jnp.mean(g * n, axis=-1, keepdims=True)
            out_ref[rows, :] = gm_ref[rows, :] + inv * back

        row_tiles(body)


def tail(g_back, w_qkv, x, gm, mod1):
    whole = lambda shape: pl.BlockSpec(shape, lambda g: (0,) * len(shape))
    return pl.pallas_call(
        tail_kernel,
        grid=(4,),
        in_specs=[
            whole((HEADS, GROWS, FR)), pl.BlockSpec((256, 3 * D), lambda g: (g, 0)),
            whole((256, D)), whole((256, D)), whole((2, 2 * D)),
        ],
        out_specs=whole((256, D)),
        out_shape=jax.ShapeDtypeStruct((256, D), F32),
        scratch_shapes=[pltpu.VMEM((4, 256, 256), F32)],
        compiler_params=pltpu.CompilerParams(vmem_limit_bytes=60 << 20),
        cost_estimate=pl.CostEstimate(flops=8 * US, bytes_accessed=10 << 20, transcendentals=0),
        name="tail",
    )(g_back, w_qkv, x, gm, mod1)


def a2a(x, axis):
    return lax.all_to_all(x, axis, 0, 0, tiled=True)


def spread(x, axis):
    n = lax.axis_size(axis)
    return a2a(jnp.broadcast_to(x[None], (n,) + x.shape), axis)


def dg(a, b, ca, cb):
    return lax.dot_general(a, b, (((ca,), (cb,)), ((), ())), preferred_element_type=F32)


def to_core(x):
    return lax.ppermute(x, "blk", [(i, i ^ 1) for i in range(NK)])


def after(x, *others):
    return lax.optimization_barrier((x,) + others)[0]


def per_device(
    frames, time_embed, segments, w_mod, b_mod, w_qkv, b_qkv, w_out, b_out,
    w_up, b_up, w_down, b_down, cotangent,
):
    R = frames.shape[0]
    blk = lax.axis_index("blk")
    bat = lax.axis_index("batch")
    core = blk % 2
    me = bat * NK + blk
    x = frames.reshape(R * FR, D)
    time_vals = time_embed.astype(F32)
    time_act, silu_back = jax.vjp(jax.nn.silu, time_vals)
    time_low = time_act.astype(BF)

    def mod_part(a, b):
        return dg(time_low, w_mod[:, a * D : b * D], 1, 0) + b_mod[a * D : b * D].astype(F32)

    inverse = jnp.exp(jnp.arange(32, dtype=F32) * (-2.0 * math.log(10000.0) / HD))
    inverse = inverse[:, None]
    mine = (blk * FR + jnp.arange(FR, dtype=jnp.int32)).astype(F32)[None, :]
    cs_me = jnp.stack([jnp.cos(mine * inverse), jnp.sin(mine * inverse)])
    qkv_send, n1, mod1 = pre(x, time_embed, b_mod.reshape(48, FR), b_qkv.reshape(24, FR), cs_me, segments, w_mod, w_qkv)
    qkv = a2a(qkv_send, "blk")

    mod2 = mod_part(2, 6)
    pos = jnp.arange(NK * FR, dtype=F32).reshape(NK, 1, FR)
    angles = pos * inverse[None]
    cs = jnp.stack([jnp.cos(angles), jnp.sin(angles)], axis=1)
    w_mod_mine = lax.dynamic_slice_in_dim(w_mod, 2 * D + blk * 256, 256, 1)

    qkv, n1_gather = lax.optimization_barrier((qkv, n1))
    norm_all = lax.all_gather(n1_gather, "blk", axis=0, tiled=False)

    o_heads, lse, edges, se = attn_fwd(qkv)
    oT = a2a(o_heads, "blk")
    output, g_middle, go_send, a_all, g_keep, g_give = mid(
        core.astype(jnp.int32).reshape(1), oT, x, cotangent.reshape(R * FR, D), mod2, b_out[None], b_up[None], b_down[None], w_out, w_up, w_down
    )
    go = a2a(go_send, "blk")

    a2_all, g2_all = to_core(a_all), to_core(g_give)
    dws = dw(a_all, a2_all, g_keep, g2_all)
    dws, go, norm_all = lax.optimization_barrier((dws, go, norm_all))
    x4 = [[4 * y + i for i in range(4)] for y in range(2)]
    dws = lax.psum_scatter(dws.reshape(NB * 256, 1280), "batch", scatter_dimension=0, axis_index_groups=x4, tiled=True)

    early = jnp.sum(go[:, 128:134].astype(F32), axis=0).reshape(3, 256).astype(BF)
    time_early = dg(early[:2], w_mod_mine, 1, 1).astype(BF)

    act_low = time_low.reshape(R, NB * NK, 8).transpose(1, 2, 0).reshape(D, R)
    act_low = jnp.pad(act_low, ((0, 0), (0, 62)))
    g_qkvT, pack = attn_bwd(
        edges, blk.astype(jnp.int32).reshape(1), qkv, se, o_heads, go, lse, cs, mod1, time_early.reshape(16, FR),
        act_low, norm_all, w_qkv
    )
    dws = after(dws, g_qkvT).reshape(2, NK, 16, 1280)
    dw_got = lax.ppermute(
        lax.dynamic_index_in_dim(dws, 1 - bat // 4, 0, keepdims=False), "batch", [(i, i ^ 4) for i in range(NB)]
    )
    dw_keep = lax.dynamic_index_in_dim(dws, bat // 4, 0, keepdims=False)
    g_back = a2a(g_qkvT, "blk")
    time_early = jnp.sum(g_back[:, 400:416].astype(F32), axis=0).reshape(R, D)
    tile = jnp.concatenate([jnp.sum(g_back[:, 384:386].astype(F32), axis=0).astype(BF), early.reshape(6, FR)], axis=0)
    tile = jnp.broadcast_to(tile[None], (NB * NK, 8, FR)).reshape(D, FR)
    pack = lax.dynamic_update_slice(pack, tile, (0, 256)).reshape(NB * NK, 8, 384)
    pack, dw_got = lax.optimization_barrier((pack, dw_got))
    dws = (dw_keep.astype(F32) + dw_got.astype(F32)).astype(BF)
    got = a2a(pack, ("batch", "blk")).reshape(NB, NK, 8, 384)
    gq = jnp.sum(got[..., :192].astype(F32), axis=0).reshape(NK, 8, 3, HD)
    grad_w_qkv = gq.transpose(1, 2, 0, 3).reshape(8, 3 * D)
    vec = got[..., 256:]
    rows_tail = vec[:, :, :2].transpose(0, 2, 1, 3).reshape(NB * R, 2 * D)
    rows_early = vec[:, :, 2:6].reshape(NB, NK, R, 2, FR).transpose(0, 2, 1, 3, 4).reshape(NB * R, 4 * D)
    rows_all = jnp.concatenate([rows_tail, rows_early], axis=1)
    act_mine = got[:, 0, :, 192:194].transpose(0, 2, 1).reshape(NB * R, 8)
    grad_w_mod = dg(act_mine, rows_all, 0, 0)
    b_mod_sum = jnp.sum(rows_all.astype(F32), axis=0)
    grad_b_mod = lax.dynamic_slice_in_dim(b_mod_sum, me * 48, 48)
    biases = jnp.sum(vec[:, :, 6:].astype(F32), axis=0).reshape(4 * D)
    grad_b_out = lax.dynamic_slice_in_dim(biases, me * 8, 8)
    grad_b_up = lax.dynamic_slice_in_dim(biases, D + me * 16, 16)
    grad_b_down = lax.dynamic_slice_in_dim(biases, 3 * D + me * 8, 8)
    b_qkv_sum = jnp.sum(got[..., 194:218].astype(F32), axis=0).transpose(0, 2, 1).reshape(NK, 3, HD)
    b_qkv_sum = b_qkv_sum.transpose(1, 0, 2).reshape(3 * D)
    grad_b_qkv = lax.dynamic_slice_in_dim(b_qkv_sum, me * 24, 24)
    rows_mine = lax.dynamic_slice_in_dim(rows_tail, bat * R, R, 0)
    (grad_time,) = silu_back(time_early + dg(rows_mine, w_mod[:, : 2 * D], 1, 1))

    dws = a2a(after(dws, got), "blk").reshape(NK // 2, 2, 16, 1280)
    dws = jnp.sum(dws.astype(F32), axis=0)
    grad_w_down = jnp.concatenate([dws[0, :, :FC], dws[1, :, :FC]], axis=1)
    grad_w_out = jnp.concatenate([dws[0, :8, FC : 2 * FC], dws[1, :8, FC : 2 * FC]], axis=1)
    grad_w_up = jnp.concatenate(
        [v for c in range(2) for v in (dws[c, 8:, FC : 2 * FC], dws[c, :8, 2 * FC :], dws[c, 8:, 2 * FC :])], axis=1
    )

    grad_frames = tail(g_back, w_qkv, x, g_middle, mod1)
    return (
        output.reshape(R, FR, D), grad_frames.reshape(R, FR, D), grad_time, grad_w_mod, grad_b_mod, grad_w_qkv,
        grad_b_qkv, grad_w_out, grad_b_out, grad_w_up, grad_b_up, grad_w_down, grad_b_down,
    )

def solution(mesh):
    both = ("batch", "blk")
    return jax.shard_map(
        per_device,
        mesh=mesh,
        in_specs=(
            P("batch", "blk", None), P("batch", None), P("batch", "blk"),
            P(), P(), P(), P(), P(), P(), P(), P(), P(), P(),
            P("batch", "blk", None),
        ),
        out_specs=(
            P("batch", "blk", None), P("batch", "blk", None), P("batch", None),
            P(both, None), P(both), P(both, None), P(both), P(both, None), P(both),
            P(both, None), P(both), P(both, None), P(both),
        ),
        check_vma=False,
    )
```

```python
import math

import jax
import jax.numpy as jnp
from jax import lax
from jax.experimental import pallas as pl
from jax.experimental.pallas import tpu as pltpu
from jax.sharding import PartitionSpec as P

BF = jnp.bfloat16
F32 = jnp.float32
NEG = -1e30
US = 1150000000
SEG = 384
GROWS = 416
LN = 128
FQ = FK = 2048
BQ = BK = 512


def dot(a, b):
    return jnp.dot(a, b, preferred_element_type=F32)


def nt(a, b):
    return lax.dot_general(a, b, (((1,), (1,)), ((), ())), preferred_element_type=F32)


def at(r, w):
    return pl.ds(pl.multiple_of((r * 3 + w) * 64, 64), 64)


def lanes(ref, j, n, *idx):
    m = n // LN
    return jnp.concatenate([ref[(j * m + i,) + idx] for i in range(m)], axis=-1)


def first_of(edge_ref, r, p):
    v = jnp.int32(0)
    for i in range(1, 6):
        e = edge_ref[r, i]
        v = jnp.where(e <= p, jnp.maximum(v, e), v)
    return v


def end_of(edge_ref, r, p):
    v = edge_ref[r, 6]
    for i in range(1, 6):
        e = edge_ref[r, i]
        v = jnp.where(e > p, jnp.minimum(v, e), v)
    return v


def over_blocks(edge_ref, r, j, size, step, make, carry):
    p0 = j * size
    p1 = p0 + size - 1
    lo = first_of(edge_ref, r, p0) // step
    hi = (end_of(edge_ref, r, p1) + step - 1) // step
    f0 = jnp.clip((first_of(edge_ref, r, p1) + step - 1) // step, lo, hi)
    f1 = jnp.clip(end_of(edge_ref, r, p0) // step, f0, hi)
    carry = lax.fori_loop(lo, f0, make(True), carry)
    carry = lax.fori_loop(f0, f1, make(False), carry)
    return lax.fori_loop(f1, hi, make(True), carry), lo, hi


def in_range(i, nk, start, end):
    kpos = i * nk + lax.broadcasted_iota(jnp.int32, (nk, start.shape[1]), 0)
    return (kpos >= start) & (kpos < end)


def fold8(x, op):
    return op(x.reshape(x.shape[0] // 8, 8, x.shape[1]), axis=0)


def segment_tables(qkv_ref, edge_ref, se_ref):
    ns = se_ref.shape[1]
    for r in range(2):
        rows = [qkv_ref[s, SEG : SEG + 16, :].astype(F32)[r : r + 1] for s in range(ns)]
        seg = jnp.concatenate(rows, axis=0)
        edge = [jnp.int32(0)] + [jnp.sum(jnp.where(seg < s, 1.0, 0.0)).astype(jnp.int32) for s in range(1, 6)]
        edge.append(jnp.int32(ns * LN))
        for i in range(7):
            edge_ref[r, i] = edge[i]
        edge_ref[r, 7] = jnp.int32(0)
        for s in range(ns):
            start = jnp.zeros((1, LN), jnp.int32)
            end = jnp.full((1, LN), edge[1], jnp.int32)
            for i in range(1, 6):
                start = jnp.where(rows[s] >= i, edge[i], start)
                end = jnp.where(rows[s] >= i, edge[i + 1], end)
            se_ref[r, s, 0:1, :] = start
            se_ref[r, s, 1:2, :] = end


def spans(se_ref, r, j, n):
    m = n // LN
    return [jnp.concatenate([se_ref[r, j * m + i, w : w + 1, :] for i in range(m)], axis=-1) for w in range(2)]


def fwd_kernel(qkv_ref, o_ref, lse_ref, edge_ref, se_ref, krow, sref):
    total = qkv_ref.shape[0] * LN
    segment_tables(qkv_ref, edge_ref, se_ref)

    def rows(r, _):
        def tr(i, _):
            krow[i] = lanes(qkv_ref, i, FK, at(r, 1)).T
            return 0

        lax.fori_loop(0, total // FK, tr, 0)

        def qblock(j, _):
            qT = lanes(qkv_ref, j, FQ, at(r, 0))
            start, end = spans(se_ref, r, j, FQ)

            def make(masked):
                def body(i, m8):
                    s = dot(krow[i], qT)
                    if masked:
                        s = jnp.where(in_range(i, FK, start, end), s, NEG)
                    sref[i] = s
                    return jnp.maximum(m8, fold8(s, jnp.max))

                return body

            m8, lo, hi = over_blocks(edge_ref, r, j, FQ, FK, make, jnp.full((8, FQ), NEG, F32))
            m = jnp.max(m8, axis=0, keepdims=True)

            def second(i, c):
                l8, acc = c
                p = jnp.exp(sref[i] - m)
                return l8 + fold8(p, jnp.sum), acc + dot(lanes(qkv_ref, i, FK, at(r, 2)), p.astype(BF))

            l8, acc = lax.fori_loop(lo, hi, second, (jnp.zeros((8, FQ), F32), jnp.zeros((64, FQ), F32)))
            l = jnp.sum(l8, axis=0, keepdims=True)
            o = (acc * (1.0 / l)).astype(BF)
            lse = m + jnp.log(l)
            for i in range(FQ // LN):
                o_ref[j * (FQ // LN) + i, r] = o[:, i * LN : (i + 1) * LN]
                lse_ref[r, j * (FQ // LN) + i] = jnp.broadcast_to(lse[:, i * LN : (i + 1) * LN], (8, LN))
            return 0

        lax.fori_loop(0, total // FQ, qblock, 0)
        return 0

    lax.fori_loop(0, 2, rows, 0)


def attn_fwd(qkv):
    ns = qkv.shape[0]
    vm = pl.BlockSpec(memory_space=pltpu.VMEM)
    S = jax.ShapeDtypeStruct
    return pl.pallas_call(
        fwd_kernel,
        in_specs=[vm],
        out_specs=[vm, vm, pl.BlockSpec(memory_space=pltpu.SMEM), vm],
        out_shape=[S((ns, 2, 64, LN), BF), S((2, ns, 8, LN), F32), S((2, 8), jnp.int32), S((2, ns, 8, LN), jnp.int32)],
        scratch_shapes=[pltpu.VMEM((ns * LN // FK, FK, 64), BF), pltpu.VMEM((ns * LN // FK, FK, FQ), F32)],
        compiler_params=pltpu.CompilerParams(vmem_limit_bytes=56 << 20),
        cost_estimate=pl.CostEstimate(flops=15 * US, bytes_accessed=3 << 20, transcendentals=8 << 20),
        name="attn_fwd",
    )(qkv)


def bwd_kernel(edge_ref, qkv_ref, se_ref, o_ref, g_ref, lse_ref, cs_ref, out_ref, kv, dq, delta):
    total = qkv_ref.shape[0] * LN

    def at_g(r):
        return pl.ds(pl.multiple_of(r * 64, 64), 64)

    def back(x, i, n):
        c, s = lanes(cs_ref, i, n, 0), lanes(cs_ref, i, n, 1)
        a, b = x[:32], x[32:]
        return jnp.concatenate([a * c + b * s, b * c - a * s], axis=0).astype(BF)

    def put(i, n, r, w, x):
        for p in range(n // LN):
            out_ref[i * (n // LN) + p, at(r, w), :] = x[:, p * LN : (p + 1) * LN]

    def row_of(ref, r, j):
        return jnp.concatenate([ref[r, j * (BQ // LN) + i, 0:1, :] for i in range(BQ // LN)], axis=-1)

    def rows(r, _):
        def prep(i, _):
            gT = g_ref[i, at_g(r), :]
            kv[pl.ds(pl.multiple_of(i * LN, LN), LN), :] = jnp.concatenate([qkv_ref[i, at(r, 1), :], qkv_ref[i, at(r, 2), :]], axis=0).T
            d = jnp.sum(gT.astype(F32) * o_ref[i, r].astype(F32), axis=0, keepdims=True)
            delta[0, i] = jnp.broadcast_to(d, (8, LN))
            return 0

        lax.fori_loop(0, total // LN, prep, 0)

        def zero(j, _):
            dq[j] = jnp.zeros((64, BQ), F32)
            return 0

        lax.fori_loop(0, total // BQ, zero, 0)

        def kblock(i, _):
            kvi = kv[pl.ds(pl.multiple_of(i * BK, BK), BK), :]
            kT = lanes(qkv_ref, i, BK, at(r, 1))
            z = jnp.zeros((64, BQ), BF)

            def make(masked):
                def body(j, c):
                    dk, dv = c
                    qT, gT = lanes(qkv_ref, j, BQ, at(r, 0)), lanes(g_ref, j, BQ, at_g(r))
                    s = dot(kvi, jnp.concatenate([qT, z], axis=0))
                    p = jnp.exp(s - row_of(lse_ref, r, j))
                    if masked:
                        start, end = spans(se_ref, r, j, BQ)
                        p = jnp.where(in_range(i, BK, start, end), p, 0.0)
                    dp = dot(kvi, jnp.concatenate([z, gT], axis=0))
                    ds = (p * (dp - row_of(delta, 0, j))).astype(BF)
                    dv = dv + nt(gT, p.astype(BF))
                    dk = dk + nt(qT, ds)
                    dq[j] = dq[j] + dot(kT, ds)
                    return dk, dv

                return body

            zz = jnp.zeros((64, BK), F32)
            (dk, dv), _, _ = over_blocks(edge_ref, r, i, BK, BQ, make, (zz, zz))
            put(i, BK, r, 1, back(dk, i, BK))
            put(i, BK, r, 2, dv.astype(BF))
            return 0

        lax.fori_loop(0, total // BK, kblock, 0)

        def fin(j, _):
            put(j, BQ, r, 0, back(dq[j] * 0.125, j, BQ))
            return 0

        lax.fori_loop(0, total // BQ, fin, 0)
        return 0

    lax.fori_loop(0, 2, rows, 0)


def attn_bwd(edges, qkv, se, o, g, lse, cs):
    ns = qkv.shape[0]
    vm = pl.BlockSpec(memory_space=pltpu.VMEM)
    V = pltpu.VMEM
    return pl.pallas_call(
        bwd_kernel,
        in_specs=[pl.BlockSpec(memory_space=pltpu.SMEM)] + [vm] * 6,
        out_specs=vm,
        out_shape=jax.ShapeDtypeStruct((ns, GROWS, LN), BF),
        scratch_shapes=[V((ns * LN, LN), BF), V((ns * LN // BQ, 64, BQ), F32), V((1, ns, 8, LN), F32)],
        compiler_params=pltpu.CompilerParams(vmem_limit_bytes=48 << 20),
        cost_estimate=pl.CostEstimate(flops=29 * US, bytes_accessed=6 << 20, transcendentals=8 << 20),
        name="attn_bwd",
    )(edges, qkv, se, o, g, lse, cs)


def wgrad_kernel(
    blk_ref, go_ref, mod_ref, act_ref, g_in, n_hbm, w_hbm, wm_hbm, g_out, gw_ref, early_ref, gv, norm, wcol, wm, extra, sem
):
    ns, width = norm.shape[0], norm.shape[2]
    total = ns * LN
    parts = 4
    each = ns // parts
    half = blk_ref[0] // 2
    bring = pltpu.make_async_copy(g_in.at[:, pl.ds(0, SEG), :], gv, sem.at[0])
    bring.start()
    chunks = [
        pltpu.make_async_copy(n_hbm.at[pl.ds(c * each, each)], norm.at[pl.ds(c * each, each)], sem.at[1 + c])
        for c in range(parts)
    ]
    for copy in chunks:
        copy.start()
    others = []
    for i in range(3):
        cols = pl.ds(pl.multiple_of(i * width + half * LN, LN), LN)
        others.append(pltpu.make_async_copy(w_hbm.at[:, cols], wcol.at[i], sem.at[5 + i]))
    cols = pl.ds(pl.multiple_of(2 * width + blk_ref[0] * 256, LN), 256)
    others.append(pltpu.make_async_copy(wm_hbm.at[:, cols], wm, sem.at[8]))
    for copy in others:
        copy.start()
    tile = go_ref[0].astype(F32)
    for i in range(1, ns):
        tile += go_ref[i].astype(F32)
    early = jnp.concatenate(
        [jnp.concatenate([tile[2 * i : 2 * i + 1], tile[2 * i + 1 : 2 * i + 2]], axis=-1) for i in range(3)]
        + [jnp.zeros((5, 256), F32)], axis=0,
    )
    early_ref[...] = early
    bring.wait()
    gt = [jnp.concatenate([gv[s, r * 192 : (r + 1) * 192, :] for s in range(ns)], axis=-1) for r in range(2)]
    m = [None, None]
    for c in range(parts):
        chunks[c].wait()
        for r in range(2):
            n = norm[c * each : (c + 1) * each, r * LN : (r + 1) * LN, :].reshape(each * LN, width)
            t = dot(gt[r][:, c * each * LN : (c + 1) * each * LN], n)
            m[r] = t if c == 0 else m[r] + t
    for copy in others:
        copy.wait()
    even = blk_ref[0] % 2 == 0
    ws = []
    for i in range(3):
        t = wcol[i].astype(F32).T
        ws.append(jnp.where(even, t[:64], t[64:]))
    w = jnp.concatenate(ws, axis=0)
    grad = jnp.zeros_like(w)
    bias = jnp.zeros((192, 1), F32)
    sums = []
    for r in range(2):
        sv = jnp.sum(gt[r].astype(F32), axis=1, keepdims=True)
        bias += sv
        grad += m[r] * (1.0 + mod_ref[r : r + 1, width:]) + sv * mod_ref[r : r + 1, :width]
        sums.append(
            jnp.concatenate([jnp.sum(w * sv, axis=0, keepdims=True), jnp.sum(w * m[r], axis=0, keepdims=True)], axis=-1)
        )
    time = nt(early[:2].astype(BF), wm[...])
    times = [time[r : r + 1, i * LN : (i + 1) * LN] for r in range(2) for i in range(width // LN)]
    times = jnp.concatenate(times, axis=0).astype(BF)
    for k in range(ns):
        mine = [v[:, k * LN : (k + 1) * LN] for v in sums] + [jnp.zeros((14, LN), F32)]
        extra[k, :16, :] = jnp.concatenate(mine, axis=0).astype(BF)
        extra[k, 16:, :] = times
    put = pltpu.make_async_copy(extra, g_out.at[:, pl.ds(SEG, GROWS - SEG), :], sem.at[9])
    put.start()
    gw_ref[:, :192] = grad.T.astype(BF)
    lane = lax.broadcasted_iota(jnp.int32, (8, 64), 1)
    column = jnp.zeros((8, 64), F32)
    for i in range(24):
        column = jnp.where(lane == 2 + i, bias[8 * i : 8 * i + 8], column)
    full = act_ref[...].astype(F32).reshape(width // 8, 8, 64) + column[None]
    gw_ref[:, 192:256] = full.reshape(width, 64).astype(BF)
    put.wait()


def wgrad(blk, go, mod1, act, g, norm, w_qkv, w_mod):
    ns = g.shape[0]
    width = w_qkv.shape[0]
    vm = pl.BlockSpec(memory_space=pltpu.VMEM)
    hbm = pl.BlockSpec(memory_space=pl.ANY)
    whole = lambda shape: pl.BlockSpec(shape, lambda s: (0,) * len(shape))
    S = jax.ShapeDtypeStruct
    V = pltpu.VMEM
    return pl.pallas_call(
        wgrad_kernel,
        grid=(1,),
        in_specs=[
            pl.BlockSpec(memory_space=pltpu.SMEM), pl.BlockSpec((ns, 16, LN), lambda s: (0, 8, 0)),
            whole(mod1.shape), whole(act.shape), hbm, hbm, hbm, hbm,
        ],
        out_specs=[hbm, whole((width, 256)), whole((8, 256))],
        out_shape=[S(g.shape, BF), S((width, 256), BF), S((8, 256), F32)],
        input_output_aliases={4: 0},
        scratch_shapes=[
            V((ns, SEG, LN), BF), V(norm.shape, BF), V((3, width, LN), BF), V((width, 256), BF),
            V((ns, GROWS - SEG, LN), BF), pltpu.SemaphoreType.DMA((10,)),
        ],
        compiler_params=pltpu.CompilerParams(vmem_limit_bytes=56 << 20),
        cost_estimate=pl.CostEstimate(flops=7 * US, bytes_accessed=12 << 20, transcendentals=0),
        name="wgrad",
    )(blk, go, mod1, act, g, norm, w_qkv, w_mod)

HEADS = 16
HD = 64
D = 1024
FF = 2048
NB = 8
NK = 16
EPS = 1e-06
FR = 128
FC = 512
RT = 32


def nt(a, b):
    return lax.dot_general(a, b, (((1,), (1,)), ((), ())), preferred_element_type=F32)


def normed(x):
    center = x - jnp.mean(x, axis=-1, keepdims=True)
    inv = lax.rsqrt(jnp.mean(center * center, axis=-1, keepdims=True) + EPS)
    return center * inv, inv


def fold(x):
    return jnp.sum(x.reshape(x.shape[0] // 8, 8, x.shape[1]), axis=0)


def row_tiles(body):
    for r in range(2):

        def step(t, _, r=r):
            body(r, pl.ds(pl.multiple_of(r * FR + t * RT, RT), RT))
            return 0

        lax.fori_loop(0, FR // RT, step, 0)


def pre_kernel(
    x_ref, t_ref, bm_ref, bq_ref, cs_ref, seg_ref, wm_hbm, wq_hbm, send_ref, n1_ref, mod_ref, wm, wq, nf, h1, sem
):
    first = pltpu.make_async_copy(wm_hbm.at[:, pl.ds(0, 2 * D)], wm, sem.at[0])
    first.start()
    copies = [
        pltpu.make_async_copy(wq_hbm.at[pl.ds(i * 256, 256), :], wq.at[pl.ds(i * 256, 256), :], sem.at[1 + i])
        for i in range(4)
    ]
    for copy in copies:
        copy.start()

    def normalize(r, rows):
        n, _ = normed(x_ref[rows, :].astype(F32))
        n1_ref[rows, :] = n.astype(BF)
        nf[rows, :] = n

    row_tiles(normalize)
    t = t_ref[...].astype(F32)
    act = (t / (1.0 + jnp.exp(-t))).astype(BF)
    bm, bq = bm_ref[:16, :].astype(F32), bq_ref[...].astype(F32)
    first.wait()
    mod_ref[...] = dot(act, wm[...]) + jnp.concatenate([bm[i : i + 1] for i in range(16)], axis=-1)

    def modulate(r, rows):
        h1[rows, :] = (nf[rows, :] * (1.0 + mod_ref[r : r + 1, D:]) + mod_ref[r : r + 1, :D]).astype(BF)

    row_tiles(modulate)
    for copy in copies:
        copy.wait()
    c = jnp.concatenate([cs_ref[0], cs_ref[0]], axis=-1)
    s = jnp.concatenate([cs_ref[1], cs_ref[1]], axis=-1)
    tile = jnp.concatenate([seg_ref[...].astype(F32), jnp.zeros((14, FR), F32)], axis=0).astype(BF)
    for g in range(4):
        for w in range(3):
            i = 4 * w + g
            p = (dot(h1[...], wq[:, i * 256 : (i + 1) * 256]) + jnp.concatenate([bq[2 * i : 2 * i + 1], bq[2 * i + 1 : 2 * i + 2]], axis=-1)).T
            for h in range(4):
                y = p[h * HD : (h + 1) * HD]
                if w < 2:
                    a, b = y[:32], y[32:]
                    y = jnp.concatenate([a * c - b * s, b * c + a * s], axis=0)
                    if w == 0:
                        y = y * 0.125
                y = y.astype(BF)
                send_ref[4 * g + h, w * HD : (w + 1) * HD, :] = y[:, :FR]
                send_ref[4 * g + h, (3 + w) * HD : (4 + w) * HD, :] = y[:, FR:]
        for h in range(4):
            send_ref[4 * g + h, SEG:, :] = tile


def pre(x, t, b_mod, b_qkv, cs_me, segments, w_mod, w_qkv):
    vm = pl.BlockSpec(memory_space=pltpu.VMEM)
    hbm = pl.BlockSpec(memory_space=pl.ANY)
    S = jax.ShapeDtypeStruct
    V = pltpu.VMEM
    return pl.pallas_call(
        pre_kernel,
        in_specs=[vm] * 6 + [hbm] * 2,
        out_specs=[vm] * 3,
        out_shape=[S((HEADS, SEG + 16, FR), BF), S((256, D), BF), S((2, 2 * D), F32)],
        scratch_shapes=[V((D, 2 * D), BF), V((D, 3 * D), BF), V((256, D), F32), V((256, D), BF), pltpu.SemaphoreType.DMA((5,))],
        compiler_params=pltpu.CompilerParams(vmem_limit_bytes=60 << 20),
        cost_estimate=pl.CostEstimate(flops=8 * US, bytes_accessed=13 << 20, transcendentals=0),
        name="pre",
    )(x, t, b_mod, b_qkv, cs_me, segments, w_mod, w_qkv)


def mid_kernel(
    core_ref, oT_ref, mod_ref, bo_ref, bu_ref, bd_ref, x_hbm, cot_hbm, wo_hbm, wu_hbm, wd_hbm,
    out_ref, gm_ref, go_ref, a_ref, keep_ref, send_ref,
    x_ref, cot_ref, wo, wu, wd, b1, mdl, n2, iv, b2, gh2, gb, sums, bsum, sem,
):
    copies = [pltpu.make_async_copy(wo_hbm, wo, sem.at[0])]
    for f in range(4):
        copies.append(pltpu.make_async_copy(wu_hbm.at[:, pl.ds(f * FC, FC)], wu.at[f], sem.at[1 + f]))
        copies.append(pltpu.make_async_copy(wd_hbm.at[pl.ds(f * FC, FC), :], wd.at[f], sem.at[5 + f]))
    rows_in = [pltpu.make_async_copy(x_hbm, x_ref, sem.at[9]), pltpu.make_async_copy(cot_hbm, cot_ref, sem.at[10])]
    for copy in copies[:1] + rows_in + copies[1:]:
        copy.start()
    low = core_ref[0] == 0

    def divide(rows, at, g):
        w = g.shape[1] // 2
        a, b = g[:, :w], g[:, w:]
        keep_ref[rows, at : at + w] = jnp.where(low, a, b)
        send_ref[rows, at : at + w] = jnp.where(low, b, a)

    sums[...] = jnp.zeros_like(sums)
    bsum[...] = jnp.zeros_like(bsum)
    o = jnp.concatenate([oT_ref[:, r].reshape(D, FR).T for r in range(2)], axis=0)
    a_ref[:, :D] = o
    copies[0].wait()
    b1[...] = dot(o, wo[...])
    for copy in rows_in:
        copy.wait()

    def first(r, rows):
        gate1, shift2 = mod_ref[r : r + 1, :D], mod_ref[r : r + 1, D : 2 * D]
        scale2, gate2 = mod_ref[r : r + 1, 2 * D : 3 * D], mod_ref[r : r + 1, 3 * D :]
        branch = b1[rows, :] + bo_ref[...].astype(F32)
        b1[rows, :] = branch
        middle = x_ref[rows, :].astype(F32) + gate1 * branch
        mdl[rows, :] = middle
        n, inv = normed(middle)
        n2[rows, :] = n
        iv[rows, :] = jnp.broadcast_to(inv, (RT, FR))
        a_ref[rows, D : 2 * D] = (n * (1.0 + scale2) + shift2).astype(BF)
        g = (gate2 * cot_ref[rows, :].astype(F32)).astype(BF)
        gb[rows, :] = g
        divide(rows, 3 * FC, g)
        bsum[:, 3 * D :] += fold(g.astype(F32))

    row_tiles(first)
    for f in range(4):
        copies[1 + 2 * f].wait()
        copies[2 + 2 * f].wait()
        u = dot(a_ref[:, D : 2 * D], wu[f]) + bu_ref[:, f * FC : (f + 1) * FC].astype(F32)
        k = math.sqrt(2.0 / math.pi)
        sq = u * u
        t = jnp.tanh(u * (k + (k * 0.044715) * sq))
        half = 0.5 * (1.0 + t)
        a = (u * half).astype(BF)
        a_ref[:, 2 * D + f * FC : 2 * D + (f + 1) * FC] = a
        slope = half + (0.5 * u) * (1.0 - t * t) * (k + (3.0 * k * 0.044715) * sq)
        gu = (nt(gb[...], wd[f]) * slope).astype(BF)
        at = FC + (f % 2) * FC

        @pl.when(low == (f < 2))
        def _(gu=gu, at=at):
            keep_ref[:, at : at + FC] = gu

        @pl.when(low != (f < 2))
        def _(gu=gu, at=at):
            send_ref[:, at : at + FC] = gu

        bsum[:, D + f * FC : D + (f + 1) * FC] += fold(gu.astype(F32))
        if f == 0:
            b2[...] = dot(a, wd[f])
            gh2[...] = nt(gu, wu[f])
        else:
            b2[...] += dot(a, wd[f])
            gh2[...] += nt(gu, wu[f])

    def last(r, rows):
        gate1, scale2, gate2 = mod_ref[r : r + 1, :D], mod_ref[r : r + 1, 2 * D : 3 * D], mod_ref[r : r + 1, 3 * D :]
        branch = b2[rows, :] + bd_ref[...].astype(F32)
        cot = cot_ref[rows, :].astype(F32)
        out_ref[rows, :] = (mdl[rows, :] + gate2 * branch).astype(BF)
        sums[r, :, 3 * D :] += fold(branch * cot)
        gh, n = gh2[rows, :], n2[rows, :]
        sums[r, :, D : 2 * D] += fold(gh)
        sums[r, :, 2 * D : 3 * D] += fold(gh * n)
        g = gh * (1.0 + scale2)
        back = g - jnp.mean(g, axis=-1, keepdims=True) - n * jnp.mean(g * n, axis=-1, keepdims=True)
        gm = cot + iv[rows, :1] * back
        gm_ref[rows, :] = gm
        sums[r, :, :D] += fold(b1[rows, :] * gm)
        g1 = (gate1 * gm).astype(BF)
        gb[rows, :] = g1
        divide(rows, 0, g1)
        bsum[:, :D] += fold(g1.astype(F32))

    row_tiles(last)
    goT = nt(wo[...], gb[...]).astype(BF)
    part = [jnp.sum(sums[r], axis=0, keepdims=True) for r in range(2)]
    bias = jnp.sum(bsum[...], axis=0, keepdims=True)
    for k in range(NK):
        go_ref[k, 0:HD] = goT[k * HD : (k + 1) * HD, :FR]
        go_ref[k, HD : 2 * HD] = goT[k * HD : (k + 1) * HD, FR:]
        at = lambda v, i: v[:, (2 * k + i) * FR : (2 * k + i + 1) * FR]
        tile = [at(part[0], 0), at(part[0], 1), at(part[1], 0), at(part[1], 1), at(bias, 0), at(bias, 1)]
        go_ref[k, 2 * HD :] = jnp.concatenate(tile + [jnp.zeros((10, FR), F32)], axis=0).astype(BF)


def mid(core, oT, x, cot, mod2, b_out, b_up, b_down, w_out, w_up, w_down):
    vm = pl.BlockSpec(memory_space=pltpu.VMEM)
    hbm = pl.BlockSpec(memory_space=pl.ANY)
    S = jax.ShapeDtypeStruct
    V = pltpu.VMEM
    return pl.pallas_call(
        mid_kernel,
        in_specs=[pl.BlockSpec(memory_space=pltpu.SMEM)] + [vm] * 5 + [hbm] * 5,
        out_specs=[vm] * 6,
        out_shape=[
            S((256, D), BF), S((256, D), F32), S((NK, 144, FR), BF), S((256, 4 * D), BF),
            S((256, 2 * D), BF), S((256, 2 * D), BF),
        ],
        scratch_shapes=[
            V((256, D), BF), V((256, D), BF), V((D, D), BF), V((4, D, FC), BF), V((4, FC, D), BF), V((256, D), F32), V((256, D), F32),
            V((256, D), F32), V((256, FR), F32), V((256, D), F32), V((256, D), F32), V((256, D), BF),
            V((2, 8, 4 * D), F32), V((8, 4 * D), F32), pltpu.SemaphoreType.DMA((11,)),
        ],
        compiler_params=pltpu.CompilerParams(vmem_limit_bytes=48 << 20),
        cost_estimate=pl.CostEstimate(flops=13 * US, bytes_accessed=16 << 20, transcendentals=256 * FF),
        name="mid",
    )(core, oT, mod2, b_out, b_up, b_down, x, cot, w_out, w_up, w_down)


def dw_kernel(oa, ob, ha, hb, aa, ab, ga, gb, out_ref):
    both = lambda a, b: jnp.concatenate([a[...].T, b[...].T], axis=-1)
    frames = lambda i, j: jnp.concatenate([ga[:, i:j], gb[:, i:j]], axis=0)
    out = dot(both(oa, ob), frames(0, FC)).reshape(NK, 8, FC)
    up = dot(both(ha, hb), frames(FC, 3 * FC)).reshape(NK, 8, 2 * FC)
    down = dot(both(aa, ab), frames(3 * FC, 4 * FC)).reshape(NK, 16, FC)
    out_ref[0, :, :, :FC] = down.astype(BF)
    out_ref[0, :, :, FC : 2 * FC] = jnp.concatenate([out, up[..., :FC]], axis=1).astype(BF)
    half = FC // 2
    out_ref[0, :, :, 2 * FC :] = jnp.concatenate([up[..., FC : FC + half], up[..., FC + half :]], axis=1).astype(BF)


def dw(a, a2, g, g2):
    cols = lambda n, first: pl.BlockSpec((256, n), lambda b: (0, first + b))
    whole = pl.BlockSpec((256, 2 * D), lambda b: (0, 0))
    return pl.pallas_call(
        dw_kernel,
        grid=(NB,),
        in_specs=[cols(128, 0)] * 2 + [cols(128, 8)] * 2 + [cols(256, 8)] * 2 + [whole] * 2,
        out_specs=pl.BlockSpec((1, NK, 16, 1280), lambda b: ((b % 4) * 2 + b // 4, 0, 0, 0)),
        out_shape=jax.ShapeDtypeStruct((NB, NK, 16, 1280), BF),
        compiler_params=pltpu.CompilerParams(vmem_limit_bytes=60 << 20),
        cost_estimate=pl.CostEstimate(flops=6 * US, bytes_accessed=12 << 20, transcendentals=0),
        name="dw",
    )(a, a2, a, a2, a, a2, g, g2)


def tail_kernel(g_ref, w_ref, x_ref, gm_ref, mod_ref, out_ref, gh1):
    step = pl.program_id(0)
    acc = None
    for w in range(3):
        g = jnp.concatenate([g_ref[:, (3 * r + w) * HD : (3 * r + w + 1) * HD, :].reshape(D, FR) for r in range(2)], axis=-1)
        t = dot(w_ref[:, w * D : (w + 1) * D], g)
        acc = t if acc is None else acc + t
    gh1[step] = acc.T

    @pl.when(step == pl.num_programs(0) - 1)
    def _():
        def body(r, rows):
            n, inv = normed(x_ref[rows, :].astype(F32))
            g = jnp.concatenate([gh1[i, rows, :] for i in range(4)], axis=-1)
            g = g * (1.0 + mod_ref[r : r + 1, D:])
            back = g - jnp.mean(g, axis=-1, keepdims=True) - n * jnp.mean(g * n, axis=-1, keepdims=True)
            out_ref[rows, :] = gm_ref[rows, :] + inv * back

        row_tiles(body)


def tail(g_back, w_qkv, x, gm, mod1):
    whole = lambda shape: pl.BlockSpec(shape, lambda g: (0,) * len(shape))
    return pl.pallas_call(
        tail_kernel,
        grid=(4,),
        in_specs=[
            whole((HEADS, GROWS, FR)), pl.BlockSpec((256, 3 * D), lambda g: (g, 0)),
            whole((256, D)), whole((256, D)), whole((2, 2 * D)),
        ],
        out_specs=whole((256, D)),
        out_shape=jax.ShapeDtypeStruct((256, D), F32),
        scratch_shapes=[pltpu.VMEM((4, 256, 256), F32)],
        compiler_params=pltpu.CompilerParams(vmem_limit_bytes=60 << 20),
        cost_estimate=pl.CostEstimate(flops=8 * US, bytes_accessed=10 << 20, transcendentals=0),
        name="tail",
    )(g_back, w_qkv, x, gm, mod1)


def a2a(x, axis):
    return lax.all_to_all(x, axis, 0, 0, tiled=True)


def spread(x, axis):
    n = lax.axis_size(axis)
    return a2a(jnp.broadcast_to(x[None], (n,) + x.shape), axis)


def dg(a, b, ca, cb):
    return lax.dot_general(a, b, (((ca,), (cb,)), ((), ())), preferred_element_type=F32)


def to_core(x):
    return lax.ppermute(x, "blk", [(i, i ^ 1) for i in range(NK)])


def after(x, *others):
    return lax.optimization_barrier((x,) + others)[0]


def per_device(
    frames, time_embed, segments, w_mod, b_mod, w_qkv, b_qkv, w_out, b_out,
    w_up, b_up, w_down, b_down, cotangent,
):
    R = frames.shape[0]
    blk = lax.axis_index("blk")
    bat = lax.axis_index("batch")
    core = blk % 2
    me = bat * NK + blk
    x = frames.reshape(R * FR, D)
    time_vals = time_embed.astype(F32)
    time_act, silu_back = jax.vjp(jax.nn.silu, time_vals)
    time_low = time_act.astype(BF)

    def mod_part(a, b):
        return dg(time_low, w_mod[:, a * D : b * D], 1, 0) + b_mod[a * D : b * D].astype(F32)

    inverse = jnp.exp(jnp.arange(32, dtype=F32) * (-2.0 * math.log(10000.0) / HD))
    inverse = inverse[:, None]
    mine = (blk * FR + jnp.arange(FR, dtype=jnp.int32)).astype(F32)[None, :]
    cs_me = jnp.stack([jnp.cos(mine * inverse), jnp.sin(mine * inverse)])
    qkv_send, n1, mod1 = pre(x, time_embed, b_mod.reshape(48, FR), b_qkv.reshape(24, FR), cs_me, segments, w_mod, w_qkv)
    qkv = a2a(qkv_send, "blk")

    mod2 = mod_part(2, 6)
    pos = jnp.arange(NK * FR, dtype=F32).reshape(NK, 1, FR)
    angles = pos * inverse[None]
    cs = jnp.stack([jnp.cos(angles), jnp.sin(angles)], axis=1)

    act_low = time_low.reshape(R, NB * NK, 8).transpose(1, 2, 0).reshape(D, R)
    act_low = jnp.pad(act_low, ((0, 0), (0, 62)))
    qkv, n1_gather, cs, act_low = lax.optimization_barrier((qkv, n1, cs, act_low))
    norm_all = lax.all_gather(n1_gather, "blk", axis=0, tiled=False)

    o_heads, lse, edges, se = attn_fwd(qkv)
    oT = a2a(o_heads, "blk")
    output, g_middle, go_send, a_all, g_keep, g_give = mid(
        core.astype(jnp.int32).reshape(1), oT, x, cotangent.reshape(R * FR, D), mod2, b_out[None], b_up[None], b_down[None], w_out, w_up, w_down
    )
    go = a2a(go_send, "blk")

    a2_all, g2_all = to_core(a_all), to_core(g_give)
    dws = dw(a_all, a2_all, g_keep, g2_all)
    dws, go = lax.optimization_barrier((dws, go))
    x4 = [[4 * y + i for i in range(4)] for y in range(2)]
    dws = lax.psum_scatter(dws.reshape(NB * 256, 1280), "batch", scatter_dimension=0, axis_index_groups=x4, tiled=True)

    g_qkvT = attn_bwd(edges, qkv, se, o_heads, go, lse, cs)
    g_qkvT, pack, early = wgrad(
        blk.astype(jnp.int32).reshape(1), go, mod1, act_low, g_qkvT, norm_all, w_qkv, w_mod
    )
    dws = after(dws, g_qkvT).reshape(2, NK, 16, 1280)
    dw_give = lax.dynamic_index_in_dim(dws, 1 - bat // 4, 0, keepdims=False)
    dw_keep = lax.dynamic_index_in_dim(dws, bat // 4, 0, keepdims=False)
    g_back = a2a(g_qkvT, "blk")
    dw_got = lax.ppermute(dw_give, "batch", [(i, i ^ 4) for i in range(NB)])

    tail_mine = jnp.sum(g_back[:, 384:386].astype(F32), axis=0).astype(BF)
    time_early = jnp.sum(g_back[:, 400:416].astype(F32), axis=0).reshape(R, D)
    tile = jnp.concatenate([tail_mine.reshape(1, 256), early[:3].astype(BF), jnp.zeros((12, 256), BF)], axis=0)
    pack = jnp.concatenate([pack.reshape(NB, FR, 256), jnp.broadcast_to(tile[None], (NB, 16, 256))], axis=1)
    pack, dw_got = lax.optimization_barrier((pack, dw_got))
    got = a2a(pack, "batch")
    w_mod_tail = lax.dynamic_slice_in_dim(w_mod, blk * FR, FR, 1)
    time_part = dg(tail_mine, w_mod_tail, 1, 1)
    gw_rows = jnp.sum(got[:, :FR, :192].astype(F32), axis=0)
    s_sum = jnp.sum(got[:, :8, 194:218].astype(F32), axis=0)
    tiles = got[:, FR : FR + 4]
    rows = jnp.concatenate([tiles[:, 0].reshape(NB * R, FR), tiles[:, 1:3].reshape(NB * R, 2 * FR)], axis=1)
    act_rows = got[:, :FR, 192:194].transpose(0, 2, 1).reshape(NB * R, FR)
    outer = dg(act_rows, rows, 0, 0)

    def wide(v, n):
        return jnp.broadcast_to(v.reshape(1, 8, n), (NK, 8, n))

    dws = dw_keep.astype(F32) + dw_got.astype(F32)
    pack3 = jnp.concatenate(
        [
            outer.reshape(NK, 8, 384),
            wide(time_part, 256),
            wide(jnp.sum(rows.astype(F32), axis=0), 48),
            wide(jnp.sum(tiles[:, 3].astype(F32), axis=0), 32),
            wide(s_sum, 24),
            gw_rows.reshape(NK, 8, 192),
            jnp.zeros((NK, 8, 88), F32),
            dws[:, :8],
            dws[:, 8:],
        ],
        axis=-1,
    ).astype(BF)
    got = a2a(pack3, "blk")
    gq = got[:, :, 744:936].astype(F32).reshape(NK, 8, 3, HD)
    grad_w_qkv = gq.transpose(1, 2, 0, 3).reshape(8, 3 * D)
    grad_w_mod = jnp.concatenate(
        [
            got[:, :, :FR].transpose(1, 0, 2).reshape(8, 2 * D),
            got[:, :, FR : 3 * FR].transpose(1, 0, 2).reshape(8, 4 * D),
        ],
        axis=1,
    ).astype(F32)
    (grad_time,) = silu_back(time_early + jnp.sum(got[:, :, 384:640].astype(F32), axis=0).reshape(R, D))
    b_mod = got[:, :, 640:688].astype(F32).reshape(NK, 384)
    b_mod_sum = jnp.concatenate([b_mod[:, :FR].reshape(-1), b_mod[:, FR:].reshape(-1)])
    grad_b_mod = lax.dynamic_slice_in_dim(b_mod_sum, me * 48, 48)
    biases = got[:, :, 688:720].astype(F32).reshape(-1)
    grad_b_out = lax.dynamic_slice_in_dim(biases, me * 8, 8)
    grad_b_up = lax.dynamic_slice_in_dim(biases, D + me * 16, 16)
    grad_b_down = lax.dynamic_slice_in_dim(biases, 3 * D + me * 8, 8)
    b_qkv_sum = got[:, :, 720:744].astype(F32).transpose(0, 2, 1).reshape(NK, 3, HD)
    b_qkv_sum = b_qkv_sum.transpose(1, 0, 2).reshape(3 * D)
    grad_b_qkv = lax.dynamic_slice_in_dim(b_qkv_sum, me * 24, 24)
    dws = jnp.sum(got[:, :, 1024:].astype(F32).reshape(NK // 2, 2, 8, 2560), axis=0)
    dws = jnp.concatenate([dws[..., :1280], dws[..., 1280:]], axis=1)
    grad_w_down = jnp.concatenate([dws[0, :, :FC], dws[1, :, :FC]], axis=1)
    grad_w_out = jnp.concatenate([dws[0, :8, FC : 2 * FC], dws[1, :8, FC : 2 * FC]], axis=1)
    grad_w_up = jnp.concatenate(
        [v for c in range(2) for v in (dws[c, 8:, FC : 2 * FC], dws[c, :8, 2 * FC :], dws[c, 8:, 2 * FC :])], axis=1
    )

    grad_frames = tail(g_back, w_qkv, x, g_middle, mod1)
    return (
        output.reshape(R, FR, D), grad_frames.reshape(R, FR, D), grad_time, grad_w_mod, grad_b_mod, grad_w_qkv,
        grad_b_qkv, grad_w_out, grad_b_out, grad_w_up, grad_b_up, grad_w_down, grad_b_down,
    )

def solution(mesh):
    both = ("batch", "blk")
    return jax.shard_map(
        per_device,
        mesh=mesh,
        in_specs=(
            P("batch", "blk", None), P("batch", None), P("batch", "blk"),
            P(), P(), P(), P(), P(), P(), P(), P(), P(), P(),
            P("batch", "blk", None),
        ),
        out_specs=(
            P("batch", "blk", None), P("batch", "blk", None), P("batch", None),
            P(both, None), P(both), P(both, None), P(both), P(both, None), P(both),
            P(both, None), P(both), P(both, None), P(both),
        ),
        check_vma=False,
    )
```
